512 devices in a mesh: row: 16 (over z_lo, x, core), col: 32 (over z_hi, y).
Axes of the slice: x: 4, y: 8, z: 8 (z_hi: 4, z_lo: 2; z = z_hi * 2 + z_lo), core: 2. Of those that a mesh axis runs over, the one named last changes fastest.
Arguments:
- amplitudes: bfloat16 [8, 2048, 2048], P(None, 'col', 'row'), may hold values from -6 to 6
- factors: bfloat16 [8, 2048, 2048], P(None, 'col'), as said below
- amp_mask: int32 [16, 16], replicated, may hold values 0 or 1
- out_mask: int32 [16, 16], replicated, may hold values 0 or 1
- partner: int32 [8], replicated, may hold values from 0 to 7, as said below
Outputs:
- residual: float32 [8, 2048, 2048], P(None, ('col', 'row'))
The draws below stay inside these ranges and needn't reach their ends.
Inputs may be any that keep to these rules, and one draw needn't show every extreme that they name: partner is an involution: partner[partner[p]] = p; exactly two pairs are their own partner. factors[q, x, y] = factors[q, y, x] for all q, x, y.
All inputs are finite; a program needn't handle non-finite values.
Results may differ from the reference program's by a relative error of at most 0.0029.
Values may be sent and summed in bfloat16 or wider, within the bound.
No kernel may reach another device: no remote copies, remote signals or barrier semaphores. Data moves between devices by JAX's collectives and lax.ppermute only.
A program may use at most 64 MiB of HBM per device.

```python
import jax
import jax.numpy as jnp
from jax import lax

P_SIZE = 8
NV = 2048
TILE = 128
QB = 8
NT = 16


def draw_partner(key, part):
    key = jax.random.fold_in(key, 7)
    shuffled = jax.random.permutation(key, P_SIZE).astype(jnp.int32)
    positions = jnp.arange(P_SIZE, dtype=jnp.int32)
    matched = jnp.where(positions < 2, positions, jnp.where(positions % 2 == 0, positions + 1, positions - 1))
    partners = jnp.zeros((P_SIZE,), jnp.int32).at[shuffled].set(shuffled[matched])
    return partners.astype(jnp.int32)


def draw_factors(key, part):
    key = jax.random.fold_in(key, 11)
    spread = (2.0 * NV) ** (-0.5)
    base = jax.random.normal(key, (QB, NV, NV), jnp.float32) * spread
    paired = (base + jnp.swapaxes(base, 1, 2)) * 0.70710678
    return paired.astype(jnp.bfloat16)


def plant(entries, key, low, largest):
    extent = entries.shape
    spot = [jax.random.randint(jax.random.fold_in(key, axis), (), 0, extent[axis]) for axis in range(len(extent))]
    entries = entries.at[tuple(spot)].set(low)
    longest = extent.index(max(extent))
    spot[longest] = (spot[longest] + 1) % extent[longest]
    return entries.at[tuple(spot)].set(largest)


def block_levels(key, extent, split, low, high):
    loudness = 1.0
    for axis_at, shards_of in split:
        draws = jax.random.uniform(jax.random.fold_in(jax.random.fold_in(key, 6), axis_at), (shards_of,), jnp.float32, low / len(split), high / len(split))
        loudness = loudness * jnp.repeat(jnp.exp(draws), extent[axis_at] // shards_of).reshape((-1,) + (1,) * (len(extent) - 1 - axis_at))
    return loudness


def bell_draw(key, dims, deviation, limit, shards=(), kind=jnp.bfloat16):
    array = jax.random.normal(key, dims, jnp.float32) * deviation
    if len(shards) > 0:
        array = block_levels(key, dims, shards, -0.22, 0.18) * array
    return jnp.clip(array, min=-limit, max=limit).astype(kind)


def setup_inputs(seed: int = 0) -> dict:
    key_list = jax.random.split(jax.random.key(seed), 6)
    amplitudes = bell_draw(key_list[0], (P_SIZE, NV, NV), 1.0, 6.0, ((1, 32), (2, 16)))
    factors = draw_factors(jax.random.fold_in(key_list[5], 71), 0)
    amp_mask = plant((jax.random.randint(key_list[2], (NT, NT), 0, 4) < 3).astype(jnp.int32), jax.random.fold_in(key_list[2], 1), 0, 1)
    out_mask = plant((jax.random.randint(key_list[3], (NT, NT), 0, 4) < 3).astype(jnp.int32), jax.random.fold_in(key_list[3], 1), 0, 1)
    partner = draw_partner(jax.random.fold_in(key_list[5], 71), 0)
    return dict(amplitudes=amplitudes, factors=factors, amp_mask=amp_mask, out_mask=out_mask, partner=partner)


def spread_tiles(occupancy):
    return jnp.repeat(jnp.repeat(occupancy, TILE, axis=0), TILE, axis=1)


def reference(amplitudes, factors, amp_mask, out_mask, partner):
    masked = amplitudes * spread_tiles(amp_mask).astype(jnp.bfloat16)
    wide_amps = masked.astype(jnp.float32)

    def one_batch(total, factor):
        block = factor.astype(jnp.float32)
        inner = jnp.einsum("ac,pcd->pad", block, wide_amps).astype(jnp.bfloat16)
        inner = lax.optimization_barrier(inner)
        return total + jnp.einsum("pad,bd->pab", inner.astype(jnp.float32), block), None

    ladder, unused_out = lax.scan(one_batch, jnp.zeros((P_SIZE, NV, NV), jnp.float32), factors)
    kept = ladder * spread_tiles(out_mask).astype(jnp.float32)
    return kept + jnp.swapaxes(kept[partner], 1, 2)
```

```python
import jax
import jax.numpy as jnp
from jax import lax
from jax.experimental import pallas as pl
from jax.experimental.pallas import tpu as pltpu
from jax.sharding import Mesh, PartitionSpec as P

ROW = ("zl", "x", "core")
COL = ("zh", "y")
ALL = ROW + COL
VMEM_LIMIT = 48 * 1024 * 1024


def params():
    return pltpu.CompilerParams(vmem_limit_bytes=VMEM_LIMIT)


def inner_kernel(own_ref, amps_ref, out_ref):
    batch_count, block_rows, width = own_ref.shape
    own = own_ref[...].reshape(batch_count * block_rows, width)
    cols = amps_ref.shape[-1]
    lanes = [amps_ref[:, :, p].reshape(width, cols) for p in range(amps_ref.shape[2])]
    product = jnp.dot(own, jnp.concatenate(lanes, axis=1), preferred_element_type=jnp.float32).astype(jnp.bfloat16)
    for p in range(len(lanes)):
        for q in range(batch_count):
            out_ref[p, :, q * cols : (q + 1) * cols] = product[
                q * block_rows : (q + 1) * block_rows, p * cols : (p + 1) * cols
            ]


def inner_call(own, amps):
    batch_count, block_rows, width = own.shape
    y_count, z_count, pair_count, rows, cols = amps.shape
    step = 2
    return pl.pallas_call(
        inner_kernel,
        grid=(pair_count // step,),
        in_specs=[
            pl.BlockSpec((batch_count, block_rows, width), lambda i: (0, 0, 0)),
            pl.BlockSpec((y_count, z_count, step, rows, cols), lambda i: (0, 0, i, 0, 0)),
        ],
        out_specs=pl.BlockSpec((step, block_rows, batch_count * cols), lambda i: (i, 0, 0)),
        out_shape=jax.ShapeDtypeStruct((pair_count, block_rows, batch_count * cols), jnp.bfloat16),
        compiler_params=params(),
    )(own, amps)


def ladder_kernel(place_ref, inner_ref, near_ref, back_ref, far_ref, ahead_ref, out_ref):
    pair_count, block_rows, depth = inner_ref.shape
    inner = inner_ref[...].reshape(pair_count * block_rows, depth)

    def emit(ref):
        blocks, batch_count, rows, cols = ref.shape
        lanes = [ref[:, q].reshape(blocks * rows, cols) for q in range(batch_count)]
        factor = jnp.concatenate(lanes, axis=1)
        product = lax.dot_general(inner, factor, (((1,), (1,)), ((), ())), preferred_element_type=jnp.float32)
        product = product.astype(jnp.bfloat16)
        for k in range(out_ref.shape[0]):
            out_ref[k] = product[:, k * 128 : (k + 1) * 128].reshape(pair_count, block_rows, 128)

    step = pl.program_id(0)
    for k, ref in enumerate((near_ref, back_ref, far_ref, ahead_ref)):
        pl.when(step // 2 == k)(lambda ref=ref: emit(ref))


def ladder_call(place, inner, parts):
    pair_count, block_rows, depth = inner.shape
    y_count, batch_count, rows, cols = parts[0].shape
    half = y_count // 2
    moves = (0, 3, 2, 1)

    def out_index(i, place):
        shift = jnp.where(i // 2 == 0, 0, 4 - i // 2)
        return (lax.rem(place[0] + shift, 4) * 2 + lax.rem(i, 2), 0, 0, 0)

    def part_spec(k):
        return pl.BlockSpec((half, batch_count, rows, cols), lambda i, place: (jnp.clip(i - 2 * k, 0, 1), 0, 0, 0))

    return pl.pallas_call(
        ladder_kernel,
        grid_spec=pltpu.PrefetchScalarGridSpec(
            num_scalar_prefetch=1,
            grid=(8,),
            in_specs=[pl.BlockSpec((pair_count, block_rows, depth), lambda i, place: (0, 0, 0))]
            + [part_spec(k) for k in range(4)],
            out_specs=pl.BlockSpec((half // 2, pair_count, block_rows, 2 * rows), out_index),
        ),
        out_shape=jax.ShapeDtypeStruct((16, pair_count, block_rows, 2 * rows), jnp.bfloat16),
        compiler_params=params(),
    )(place, inner, *parts)


def reduce_kernel(info_ref, part_ref, kept_ref, same_ref, other_ref):
    weight = info_ref[0].astype(jnp.float32)
    side = info_ref[1]
    halves = []
    for p in range(2):
        total = part_ref[0, p].astype(jnp.float32)
        for k in range(1, part_ref.shape[0]):
            total = total + part_ref[k, p].astype(jnp.float32)
        total = total * weight
        kept_ref[p] = total
        halves.append(total.T)
    turned = jnp.concatenate(halves, axis=1).astype(jnp.bfloat16)
    low, high = turned[:64], turned[64:]
    same_ref[0] = jnp.where(side == 0, low, high)
    other_ref[0] = jnp.where(side == 0, high, low)


def reduce_call(info, pieces):
    sources, pair_count, rows, cols = pieces.shape
    return pl.pallas_call(
        reduce_kernel,
        grid_spec=pltpu.PrefetchScalarGridSpec(
            num_scalar_prefetch=1,
            grid=(pair_count // 2,),
            in_specs=[pl.BlockSpec((sources, 2, rows, cols), lambda i, info: (0, i, 0, 0))],
            out_specs=[
                pl.BlockSpec((2, rows, cols), lambda i, info: (i, 0, 0)),
                pl.BlockSpec((1, rows, cols), lambda i, info: (i, 0, 0)),
                pl.BlockSpec((1, rows, cols), lambda i, info: (i, 0, 0)),
            ],
        ),
        out_shape=[
            jax.ShapeDtypeStruct((pair_count, rows, cols), jnp.float32),
            jax.ShapeDtypeStruct((pair_count // 2, rows, cols), jnp.bfloat16),
            jax.ShapeDtypeStruct((pair_count // 2, rows, cols), jnp.bfloat16),
        ],
        compiler_params=params(),
    )(info, pieces)


def combine_kernel(info_ref, partner_ref, kept_ref, same_ref, other_ref, out_ref):
    side = info_ref[1]
    pair_count, rows, cols = kept_ref.shape
    half = cols // 2
    for p in range(pair_count):
        mate = partner_ref[p]
        odd = lax.rem(mate, 2) == 1
        same = same_ref[mate // 2].astype(jnp.float32)
        other = other_ref[mate // 2].astype(jnp.float32)
        same = jnp.where(odd, same[:, half:], same[:, :half])
        other = jnp.where(odd, other[:, half:], other[:, :half])
        first = jnp.where(side == 0, same, other)
        second = jnp.where(side == 0, other, same)
        total = kept_ref[p] + jnp.concatenate([first, second], axis=1)
        for k in range(16):
            out_ref[k, p * 4 : (p + 1) * 4, :] = total[k * 4 : (k + 1) * 4]


def combine_call(info, partner, kept, same, other):
    pair_count, rows, cols = kept.shape
    smem = pl.BlockSpec(memory_space=pltpu.SMEM)
    vmem = pl.BlockSpec(memory_space=pltpu.VMEM)
    return pl.pallas_call(
        combine_kernel,
        in_specs=[smem, smem, vmem, vmem, vmem],
        out_specs=vmem,
        out_shape=jax.ShapeDtypeStruct((16, pair_count * rows // 16, cols), jnp.float32),
        compiler_params=params(),
    )(info, partner, kept, same, other)


def turn(count, step):
    return [(i, (i + step) % count) for i in range(count)]


def mirror_pairs(other):
    pairs = []
    for r in range(16):
        for c in range(32):
            side = 1 - c % 2 if other else c % 2
            pairs.append((r * 32 + c, (c // 2) * 32 + 2 * r + side))
    return pairs


def on_device(amplitudes, factors, amp_mask, out_mask, partner):
    pair_count, amp_rows, amp_cols = amplitudes.shape
    batch_count, block_rows, full_width = factors.shape
    r = lax.axis_index(ROW)
    c = lax.axis_index(COL)
    zh = lax.axis_index("zh")
    masked = amplitudes * amp_mask[c // 2, r].astype(jnp.bfloat16)

    block = lax.dynamic_slice_in_dim(factors, r * amp_cols, amp_cols, 2)
    near = lax.all_gather(block, "y", axis=0)
    amps = lax.all_gather(lax.all_gather(masked, "zh", axis=0), "y", axis=0)

    back = lax.ppermute(near, "zh", turn(4, 1))
    ahead = lax.ppermute(near, "zh", turn(4, -1))
    far = jnp.concatenate(
        [lax.ppermute(back[:4], "zh", turn(4, 1)), lax.ppermute(ahead[4:], "zh", turn(4, -1))], axis=0
    )
    own = factors.reshape(batch_count, block_rows, 4, 8, 64).transpose(0, 1, 3, 2, 4)
    own = own.reshape(batch_count, block_rows, full_width)

    inner = inner_call(own, amps)
    partial = ladder_call(zh.reshape(1), inner, (near, back, far, ahead))
    pieces = lax.all_to_all(partial, ROW, split_axis=0, concat_axis=0)
    info = jnp.stack([out_mask[c // 2, r], c % 2])
    kept, same, other = reduce_call(info, pieces)
    same = lax.ppermute(same, ALL, mirror_pairs(False))
    other = lax.ppermute(other, ALL, mirror_pairs(True))
    rows = lax.all_to_all(combine_call(info, partner, kept, same, other), ROW, split_axis=0, concat_axis=0)
    rows = rows.reshape(16, pair_count, 4, 128).transpose(1, 2, 0, 3)
    return rows.reshape(pair_count, 4, full_width)


def solution(mesh):
    fine = Mesh(mesh.devices.reshape(2, 4, 2, 4, 8), ALL)
    return jax.shard_map(
        on_device,
        mesh=fine,
        in_specs=(P(None, COL, ROW), P(None, COL, None), P(), P(), P()),
        out_specs=P(None, COL + ROW, None),
        check_vma=False,
    )
```

```python
import jax
import jax.numpy as jnp
from jax import lax
from jax.experimental import pallas as pl
from jax.experimental.pallas import tpu as pltpu
from jax.sharding import Mesh, PartitionSpec as P

ROW = ("zl", "x", "core")
COL = ("zh", "y")
ALL = ROW + COL
VMEM_LIMIT = 48 * 1024 * 1024


def params():
    return pltpu.CompilerParams(vmem_limit_bytes=VMEM_LIMIT)


def prepare_kernel(info_ref, amps_ref, factor_ref, first_ref, second_ref):
    weight = info_ref[0].astype(jnp.bfloat16)
    batch_count = factor_ref.shape[0]
    ring = second_ref.shape[1]
    first_ref[:batch_count] = factor_ref[...]
    first_ref[batch_count:] = amps_ref[ring:] * weight
    masked = amps_ref[:ring] * weight
    for k in range(second_ref.shape[0]):
        second_ref[k] = masked


def prepare_call(info, amplitudes, factors, ring, copies):
    pair_count, rows, cols = amplitudes.shape
    batch_count = factors.shape[0]
    flat = batch_count + pair_count - ring
    return pl.pallas_call(
        prepare_kernel,
        grid_spec=pltpu.PrefetchScalarGridSpec(
            num_scalar_prefetch=1,
            grid=(1,),
            in_specs=[
                pl.BlockSpec((pair_count, rows, cols), lambda i, info: (0, 0, 0)),
                pl.BlockSpec((batch_count, rows, cols), lambda i, info: (0, 0, info[1])),
            ],
            out_specs=[
                pl.BlockSpec((flat, rows, cols), lambda i, info: (0, 0, 0)),
                pl.BlockSpec((copies, ring, rows, cols), lambda i, info: (0, 0, 0, 0)),
            ],
        ),
        out_shape=[
            jax.ShapeDtypeStruct((flat, rows, cols), jnp.bfloat16),
            jax.ShapeDtypeStruct((copies, ring, rows, cols), jnp.bfloat16),
        ],
        compiler_params=params(),
    )(info, amplitudes, factors)


def spread_product(product, out_ref, batch_count, block_rows, cols):
    product = product.astype(jnp.bfloat16)
    for p in range(out_ref.shape[0]):
        for q in range(batch_count):
            out_ref[p, :, q * cols : (q + 1) * cols] = product[
                q * block_rows : (q + 1) * block_rows, p * cols : (p + 1) * cols
            ]


def ring_kernel(place_ref, own_ref, near_ref, back_ref, ahead_ref, left_ref, right_ref, out_ref):
    batch_count, block_rows, width = own_ref.shape
    cols = near_ref.shape[-1]
    group = width // 4

    def term(blocks, move):
        at = pl.multiple_of(lax.rem(place_ref[0] + move, 4) * group, group)
        own = own_ref[:, :, pl.ds(at, group)].reshape(batch_count * block_rows, group)
        lanes = [jnp.concatenate([ref[k, p] for ref in blocks for k in range(ref.shape[0])], axis=0) for p in range(2)]
        return jnp.dot(own, jnp.concatenate(lanes, axis=1), preferred_element_type=jnp.float32)

    product = term([near_ref], 0)
    product = product + term([back_ref], 3)
    product = product + term([ahead_ref], 1)
    product = product + term([left_ref, right_ref], 2)
    spread_product(product, out_ref, batch_count, block_rows, cols)


def ring_call(place, own, parts):
    batch_count, block_rows, width = own.shape
    pair_count, rows, cols = parts[0].shape[1:]
    return pl.pallas_call(
        ring_kernel,
        grid_spec=pltpu.PrefetchScalarGridSpec(
            num_scalar_prefetch=1,
            grid=(pair_count // 2,),
            in_specs=[pl.BlockSpec((batch_count, block_rows, width), lambda i, place: (0, 0, 0))]
            + [pl.BlockSpec((part.shape[0], 2, rows, cols), lambda i, place: (0, i, 0, 0)) for part in parts],
            out_specs=pl.BlockSpec((2, block_rows, batch_count * cols), lambda i, place: (i, 0, 0)),
        ),
        out_shape=jax.ShapeDtypeStruct((pair_count, block_rows, batch_count * cols), jnp.bfloat16),
        compiler_params=params(),
    )(place, own, *parts)


def flat_kernel(own_ref, amps_ref, out_ref):
    batch_count, block_rows, width = own_ref.shape
    y_count, z_count, pairs, rows, cols = amps_ref.shape
    own = own_ref[...].reshape(batch_count * block_rows, width)
    lanes = [
        jnp.concatenate([amps_ref[y, z, p] for z in range(z_count) for y in range(y_count)], axis=0)
        for p in range(pairs)
    ]
    product = jnp.dot(own, jnp.concatenate(lanes, axis=1), preferred_element_type=jnp.float32)
    spread_product(product, out_ref, batch_count, block_rows, cols)


def flat_call(own, units):
    batch_count, block_rows, width = own.shape
    y_count, z_count, unit_count, rows, cols = units.shape
    return pl.pallas_call(
        flat_kernel,
        grid=(1,),
        in_specs=[
            pl.BlockSpec((batch_count, block_rows, width), lambda i: (0, 0, 0)),
            pl.BlockSpec((y_count, z_count, 2, rows, cols), lambda i: (0, 0, batch_count // 2, 0, 0)),
        ],
        out_specs=pl.BlockSpec((2, block_rows, batch_count * cols), lambda i: (0, 0, 0)),
        out_shape=jax.ShapeDtypeStruct((2, block_rows, batch_count * cols), jnp.bfloat16),
        compiler_params=params(),
    )(own, units)


def ladder_kernel(core_ref, ring_ref, flat_ref, units_ref, keep_ref, send_ref):
    y_count, z_count, batch_count, rows, cols = units_ref.shape
    pair_count, block_rows = keep_ref.shape[1:3]
    depth = ring_ref.shape[2]
    inner = jnp.concatenate([ring_ref[...].reshape(-1, depth), flat_ref[...].reshape(-1, depth)], axis=0)
    lanes = [jnp.concatenate([units_ref[y, 0, q] for y in range(y_count)], axis=0) for q in range(batch_count)]
    factor = jnp.concatenate(lanes, axis=1)
    product = lax.dot_general(inner, factor, (((1,), (1,)), ((), ())), preferred_element_type=jnp.float32)
    half = product.shape[1] // 2
    first = product[:, :half].reshape(pair_count, block_rows, half)
    second = product[:, half:].reshape(pair_count, block_rows, half)
    own_first = core_ref[0] == 0
    keep_ref[0] = jnp.where(own_first, first, second)
    send_ref[0] = jnp.where(own_first, second, first).astype(jnp.bfloat16)


def ladder_call(core, ring, flat, units):
    depth = ring.shape[2]
    block_rows = ring.shape[1]
    pair_count = ring.shape[0] + flat.shape[0]
    y_count, z_count, unit_count, rows, cols = units.shape
    batch_count = depth // cols
    half = y_count // 2
    out_spec = pl.BlockSpec((1, pair_count, block_rows, 2 * rows), lambda i, core: (i, 0, 0, 0))
    return pl.pallas_call(
        ladder_kernel,
        grid_spec=pltpu.PrefetchScalarGridSpec(
            num_scalar_prefetch=1,
            grid=(8,),
            in_specs=[
                pl.BlockSpec(ring.shape, lambda i, core: (0, 0, 0)),
                pl.BlockSpec(flat.shape, lambda i, core: (0, 0, 0)),
                pl.BlockSpec((half, 1, batch_count, rows, cols), lambda i, core: (i % 2, i // 2, 0, 0, 0)),
            ],
            out_specs=[out_spec, out_spec],
        ),
        out_shape=[
            jax.ShapeDtypeStruct((8, pair_count, block_rows, 2 * rows), jnp.float32),
            jax.ShapeDtypeStruct((8, pair_count, block_rows, 2 * rows), jnp.bfloat16),
        ],
        compiler_params=params(),
    )(core, ring, flat, units)


def reduce_kernel(info_ref, part_ref, kept_ref, same_ref, other_ref):
    weight = info_ref[0].astype(jnp.float32)
    side = info_ref[1]
    halves = []
    for p in range(2):
        total = part_ref[0, p].astype(jnp.float32)
        for k in range(1, part_ref.shape[0]):
            total = total + part_ref[k, p].astype(jnp.float32)
        total = total * weight
        kept_ref[p] = total
        halves.append(total.T)
    turned = jnp.concatenate(halves, axis=1).astype(jnp.bfloat16)
    low, high = turned[:64], turned[64:]
    same_ref[0] = jnp.where(side == 0, low, high)
    other_ref[0] = jnp.where(side == 0, high, low)


def reduce_call(info, pieces):
    sources, pair_count, rows, cols = pieces.shape
    return pl.pallas_call(
        reduce_kernel,
        grid_spec=pltpu.PrefetchScalarGridSpec(
            num_scalar_prefetch=1,
            grid=(pair_count // 2,),
            in_specs=[pl.BlockSpec((sources, 2, rows, cols), lambda i, info: (0, i, 0, 0))],
            out_specs=[
                pl.BlockSpec((2, rows, cols), lambda i, info: (i, 0, 0)),
                pl.BlockSpec((1, rows, cols), lambda i, info: (i, 0, 0)),
                pl.BlockSpec((1, rows, cols), lambda i, info: (i, 0, 0)),
            ],
        ),
        out_shape=[
            jax.ShapeDtypeStruct((pair_count, rows, cols), jnp.float32),
            jax.ShapeDtypeStruct((pair_count // 2, rows, cols), jnp.bfloat16),
            jax.ShapeDtypeStruct((pair_count // 2, rows, cols), jnp.bfloat16),
        ],
        compiler_params=params(),
    )(info, pieces)


def combine_kernel(info_ref, partner_ref, kept_ref, same_ref, other_ref, out_ref):
    side = info_ref[1]
    pair_count, rows, cols = kept_ref.shape
    half = cols // 2
    for p in range(pair_count):
        mate = partner_ref[p]
        odd = lax.rem(mate, 2) == 1
        same = same_ref[mate // 2].astype(jnp.float32)
        other = other_ref[mate // 2].astype(jnp.float32)
        same = jnp.where(odd, same[:, half:], same[:, :half])
        other = jnp.where(odd, other[:, half:], other[:, :half])
        first = jnp.where(side == 0, same, other)
        second = jnp.where(side == 0, other, same)
        total = kept_ref[p] + jnp.concatenate([first, second], axis=1)
        for k in range(16):
            out_ref[k, p * 4 : (p + 1) * 4, :] = total[k * 4 : (k + 1) * 4]


def combine_call(info, partner, kept, same, other):
    pair_count, rows, cols = kept.shape
    smem = pl.BlockSpec(memory_space=pltpu.SMEM)
    vmem = pl.BlockSpec(memory_space=pltpu.VMEM)
    return pl.pallas_call(
        combine_kernel,
        in_specs=[smem, smem, vmem, vmem, vmem],
        out_specs=vmem,
        out_shape=jax.ShapeDtypeStruct((16, pair_count * rows // 16, cols), jnp.float32),
        compiler_params=params(),
    )(info, partner, kept, same, other)


def turn(count, step):
    return [(i, (i + step) % count) for i in range(count)]


def mirror_pairs(other):
    pairs = []
    for r in range(16):
        for c in range(32):
            side = 1 - c % 2 if other else c % 2
            pairs.append((r * 32 + c, (c // 2) * 32 + 2 * r + side))
    return pairs


def on_device(amplitudes, factors, amp_mask, out_mask, partner):
    pair_count, amp_rows, amp_cols = amplitudes.shape
    batch_count, block_rows, full_width = factors.shape
    r = lax.axis_index(ROW)
    c = lax.axis_index(COL)
    zh = lax.axis_index("zh")
    core = lax.axis_index("core")
    ring = 6
    first, second = prepare_call(jnp.stack([amp_mask[c // 2, r], r]), amplitudes, factors, ring, 8)
    near = lax.all_to_all(second, "y", split_axis=0, concat_axis=0)
    units = lax.all_gather(lax.all_gather(first, "zh", axis=0), "y", axis=0)

    back = lax.ppermute(near, "zh", turn(4, 1))
    ahead = lax.ppermute(near, "zh", turn(4, -1))
    left = lax.ppermute(back[:4], "zh", turn(4, 1))
    right = lax.ppermute(ahead[4:], "zh", turn(4, -1))

    ring_inner = ring_call(zh.reshape(1), factors, (near, back, ahead, left, right))
    flat_inner = flat_call(factors, units)
    keep, send = ladder_call(core.reshape(1), ring_inner, flat_inner, units)
    swapped = lax.ppermute(send, "core", turn(2, 1))
    partial = (keep + swapped.astype(jnp.float32)).astype(jnp.bfloat16)
    pieces = lax.all_to_all(partial, ("zl", "x"), split_axis=0, concat_axis=0)
    info = jnp.stack([out_mask[c // 2, r], c % 2])
    kept, same, other = reduce_call(info, pieces)
    same = lax.ppermute(same, ALL, mirror_pairs(False))
    other = lax.ppermute(other, ALL, mirror_pairs(True))
    rows = lax.all_to_all(combine_call(info, partner, kept, same, other), ROW, split_axis=0, concat_axis=0)
    rows = rows.reshape(16, pair_count, 4, 128).transpose(1, 2, 0, 3)
    return rows.reshape(pair_count, 4, full_width)


def solution(mesh):
    fine = Mesh(mesh.devices.reshape(2, 4, 2, 4, 8), ALL)
    return jax.shard_map(
        on_device,
        mesh=fine,
        in_specs=(P(None, COL, ROW), P(None, COL, None), P(), P(), P()),
        out_specs=P(None, COL + ROW, None),
        check_vma=False,
    )
```

```python
import jax
import jax.numpy as jnp
from jax import lax
from jax.experimental import pallas as pl
from jax.experimental.pallas import tpu as pltpu
from jax.sharding import Mesh, PartitionSpec as P

ROW = ("zl", "x", "core")
COL = ("zh", "y")
ALL = ROW + COL
MIB = 1024 * 1024


def params(mib=16):
    return pltpu.CompilerParams(vmem_limit_bytes=mib * MIB)


def place(names):
    at = lax.axis_index(names[0])
    for name in names[1:]:
        at = at * lax.axis_size(name) + lax.axis_index(name)
    return at


def prepare_kernel(mask_ref, amps_ref, factor_ref, first_ref, second_ref, copy_sem):
    batch_count, ring = factor_ref.shape[0], second_ref.shape[1]
    r = place(ROW)
    cols = amps_ref.shape[2]
    block = factor_ref.at[:, :, pl.ds(pl.multiple_of(r * cols, cols), cols)]
    copy = pltpu.make_async_copy(block, first_ref.at[:batch_count], copy_sem)
    copy.start()
    weight = mask_ref[place(COL) // 2, r].astype(jnp.float32).astype(jnp.bfloat16)
    masked = amps_ref[:ring] * weight
    for k in range(second_ref.shape[0]):
        second_ref[k] = masked
    first_ref[batch_count:] = amps_ref[ring:] * weight
    copy.wait()


def prepare_call(mask, amplitudes, factors, ring, copies):
    pair_count, rows, cols = amplitudes.shape
    flat = factors.shape[0] + pair_count - ring
    vmem = pl.BlockSpec(memory_space=pltpu.VMEM)
    return pl.pallas_call(
        prepare_kernel,
        in_specs=[pl.BlockSpec(memory_space=pltpu.SMEM), vmem, pl.BlockSpec(memory_space=pltpu.HBM)],
        out_specs=[vmem, vmem],
        out_shape=[
            jax.ShapeDtypeStruct((flat, rows, cols), jnp.bfloat16),
            jax.ShapeDtypeStruct((copies, ring, rows, cols), jnp.bfloat16),
        ],
        scratch_shapes=[pltpu.SemaphoreType.DMA],
        compiler_params=params(60),
    )(mask, amplitudes, factors)


def gate_kernel(held_ref, other_ref, out_ref):
    pass


def gate_call(held, other):
    anywhere = pl.BlockSpec(memory_space=pl.ANY)
    return pl.pallas_call(
        gate_kernel,
        in_specs=[anywhere, anywhere],
        out_specs=anywhere,
        out_shape=jax.ShapeDtypeStruct(held.shape, held.dtype),
        input_output_aliases={0: 0},
        compiler_params=params(),
    )(held, other)


def spread_product(product, out_ref, first, batch_count, block_rows):
    product = product.astype(jnp.bfloat16)
    cols = out_ref.shape[2] // batch_count
    for p in range(product.shape[1] // cols):
        for q in range(batch_count):
            out_ref[first + p, :, q * cols : (q + 1) * cols] = product[
                q * block_rows : (q + 1) * block_rows, p * cols : (p + 1) * cols
            ]


def ring_term(own_ref, blocks, move):
    batch_count, block_rows, width = own_ref.shape
    group = width // 4
    at = pl.multiple_of(lax.rem(lax.axis_index("zh") + move, 4) * group, group)
    own = own_ref[:, :, pl.ds(at, group)].reshape(batch_count * block_rows, group)
    lanes = [
        jnp.concatenate([ref[k, p] for ref in blocks for k in range(ref.shape[0])], axis=0)
        for p in range(blocks[0].shape[1])
    ]
    return jnp.dot(own, jnp.concatenate(lanes, axis=1), preferred_element_type=jnp.float32)


def early_kernel(own_ref, near_ref, back_ref, ahead_ref, out_ref):
    product = ring_term(own_ref, [near_ref], 0)
    product = product + ring_term(own_ref, [back_ref], 3)
    out_ref[...] = product + ring_term(own_ref, [ahead_ref], 1)


def early_call(own, parts):
    batch_count, block_rows, width = own.shape
    pair_count, rows, cols = parts[0].shape[1:]
    return pl.pallas_call(
        early_kernel,
        grid=(pair_count // 2,),
        in_specs=[pl.BlockSpec(memory_space=pltpu.VMEM)]
        + [pl.BlockSpec((part.shape[0], 2, rows, cols), lambda i: (0, i, 0, 0)) for part in parts],
        out_specs=pl.BlockSpec((batch_count * block_rows, 2 * cols), lambda i: (0, i)),
        out_shape=jax.ShapeDtypeStruct((batch_count * block_rows, pair_count * cols), jnp.float32),
        compiler_params=params(),
    )(own, *parts)


def late_kernel(own_ref, left_ref, right_ref, early_ref, out_ref):
    batch_count, block_rows, width = own_ref.shape
    product = early_ref[...] + ring_term(own_ref, [left_ref, right_ref], 2)
    spread_product(product, out_ref, 0, batch_count, block_rows)


def late_call(own, parts, early):
    batch_count, block_rows, width = own.shape
    pair_count, rows, cols = parts[0].shape[1:]
    vmem = pl.BlockSpec(memory_space=pltpu.VMEM)
    return pl.pallas_call(
        late_kernel,
        in_specs=[vmem] * 4,
        out_specs=vmem,
        out_shape=jax.ShapeDtypeStruct((pair_count, block_rows, batch_count * cols), jnp.bfloat16),
        compiler_params=params(),
    )(own, *parts, early)


def ladder_term(inner_ref, low_ref, high_ref, out_ref):
    y_count, z_count, batch_count, rows, cols = low_ref.shape
    pair_count, block_rows, depth = inner_ref.shape
    inner = inner_ref[...].reshape(pair_count * block_rows, depth)
    lanes = [
        jnp.concatenate([ref[y, 0, q] for ref in (low_ref, high_ref) for y in range(y_count)], axis=0)
        for q in range(batch_count)
    ]
    factor = jnp.concatenate(lanes, axis=1)
    product = lax.dot_general(inner, factor, (((1,), (1,)), ((), ())), preferred_element_type=jnp.float32)
    half = product.shape[1] // 2
    for k in range(2):
        out_ref[k] = product[:, k * half : (k + 1) * half].reshape(pair_count, block_rows, half).astype(out_ref.dtype)


def send_kernel(side_ref, own_ref, ring_ref, *refs):
    amps_refs, (low_ref, high_ref, out_ref, inner_ref) = refs[:-4], refs[-4:]
    batch_count, block_rows, width = own_ref.shape
    ring = ring_ref.shape[0]

    @pl.when(pl.program_id(0) == 0)
    def _():
        inner_ref[:ring] = ring_ref[...]
        own = own_ref[...].reshape(batch_count * block_rows, width)
        lanes = [
            jnp.concatenate([ref[y, z, 0] for z in range(ref.shape[1]) for y in range(ref.shape[0])], axis=0)
            for ref in amps_refs
        ]
        product = jnp.dot(own, jnp.concatenate(lanes, axis=1), preferred_element_type=jnp.float32)
        spread_product(product, inner_ref, ring, batch_count, block_rows)

    pl.when(pl.program_id(0) > 0)(lambda: ladder_term(inner_ref, low_ref, high_ref, out_ref))


def send_call(side, own, ring_inner, units):
    ring, block_rows, depth = ring_inner.shape
    y_count, z_count, unit_count, rows, cols = units.shape
    batch_count = depth // cols
    flat = unit_count - batch_count
    pair_count = ring + flat
    quarter = (y_count // 4, 1, batch_count, rows, cols)

    def amps_spec(k):
        return pl.BlockSpec((y_count, z_count, 1, rows, cols), lambda i, side: (0, 0, batch_count + k, 0, 0))

    return pl.pallas_call(
        send_kernel,
        grid_spec=pltpu.PrefetchScalarGridSpec(
            num_scalar_prefetch=1,
            grid=(z_count + 1,),
            in_specs=[
                pl.BlockSpec(memory_space=pltpu.VMEM),
                pl.BlockSpec(memory_space=pltpu.VMEM),
            ]
            + [amps_spec(k) for k in range(flat)]
            + [
                pl.BlockSpec(quarter, lambda i, side: (side[0], jnp.maximum(i - 1, 0), 0, 0, 0)),
                pl.BlockSpec(quarter, lambda i, side: (side[0] + 2, jnp.maximum(i - 1, 0), 0, 0, 0)),
            ],
            out_specs=[
                pl.BlockSpec((2, pair_count, block_rows, 2 * rows), lambda i, side: (jnp.maximum(i - 1, 0), 0, 0, 0)),
                pl.BlockSpec((pair_count, block_rows, depth), lambda i, side: (0, 0, 0)),
            ],
        ),
        out_shape=[
            jax.ShapeDtypeStruct((8, pair_count, block_rows, 2 * rows), jnp.bfloat16),
            jax.ShapeDtypeStruct((pair_count, block_rows, depth), jnp.bfloat16),
        ],
        compiler_params=params(48),
    )(side, own, ring_inner, *[units] * (flat + 2))


def keep_kernel(side_ref, inner_ref, low_ref, high_ref, out_ref):
    ladder_term(inner_ref, low_ref, high_ref, out_ref)


def keep_call(side, inner, units):
    pair_count, block_rows, depth = inner.shape
    y_count, z_count, unit_count, rows, cols = units.shape
    quarter = (y_count // 4, 1, depth // cols, rows, cols)
    return pl.pallas_call(
        keep_kernel,
        grid_spec=pltpu.PrefetchScalarGridSpec(
            num_scalar_prefetch=1,
            grid=(z_count,),
            in_specs=[
                pl.BlockSpec(memory_space=pltpu.VMEM),
                pl.BlockSpec(quarter, lambda i, side: (side[0], i, 0, 0, 0)),
                pl.BlockSpec(quarter, lambda i, side: (side[0] + 2, i, 0, 0, 0)),
            ],
            out_specs=pl.BlockSpec((2, pair_count, block_rows, 2 * rows), lambda i, side: (i, 0, 0, 0)),
        ),
        out_shape=jax.ShapeDtypeStruct((8, pair_count, block_rows, 2 * rows), jnp.float32),
        compiler_params=params(48),
    )(side, inner, units, units)


def reduce_kernel(mask_ref, part_ref, kept_ref, same_ref, other_ref):
    c = place(COL)
    weight = mask_ref[c // 2, place(ROW)].astype(jnp.float32)
    side = lax.rem(c, 2)
    halves = []
    for p in range(2):
        total = part_ref[0, p].astype(jnp.float32)
        for k in range(1, part_ref.shape[0]):
            total = total + part_ref[k, p].astype(jnp.float32)
        total = total * weight
        kept_ref[p] = total
        halves.append(total.T)
    turned = jnp.concatenate(halves, axis=1).astype(jnp.bfloat16)
    low, high = turned[:64], turned[64:]
    same_ref[0] = jnp.where(side == 0, low, high)
    other_ref[0] = jnp.where(side == 0, high, low)


def reduce_call(mask, pieces):
    sources, pair_count, rows, cols = pieces.shape
    half_spec = pl.BlockSpec((1, rows, cols), lambda i: (i, 0, 0))
    return pl.pallas_call(
        reduce_kernel,
        grid=(pair_count // 2,),
        in_specs=[
            pl.BlockSpec(memory_space=pltpu.SMEM),
            pl.BlockSpec((sources, 2, rows, cols), lambda i: (0, i, 0, 0)),
        ],
        out_specs=[pl.BlockSpec((2, rows, cols), lambda i: (i, 0, 0)), half_spec, half_spec],
        out_shape=[
            jax.ShapeDtypeStruct((pair_count, rows, cols), jnp.float32),
            jax.ShapeDtypeStruct((pair_count // 2, rows, cols), jnp.bfloat16),
            jax.ShapeDtypeStruct((pair_count // 2, rows, cols), jnp.bfloat16),
        ],
        compiler_params=params(),
    )(mask, pieces)


def combine_kernel(partner_ref, kept_ref, same_ref, other_ref, out_ref):
    side = lax.rem(place(COL), 2)
    pair_count, rows, cols = kept_ref.shape
    half = cols // 2
    for p in range(pair_count):
        mate = partner_ref[p]
        odd = lax.rem(mate, 2) == 1
        same = same_ref[mate // 2].astype(jnp.float32)
        other = other_ref[mate // 2].astype(jnp.float32)
        same = jnp.where(odd, same[:, half:], same[:, :half])
        other = jnp.where(odd, other[:, half:], other[:, :half])
        first = jnp.where(side == 0, same, other)
        second = jnp.where(side == 0, other, same)
        total = kept_ref[p] + jnp.concatenate([first, second], axis=1)
        for k in range(16):
            out_ref[k, p * 4 : (p + 1) * 4, :] = total[k * 4 : (k + 1) * 4]


def combine_call(partner, kept, same, other):
    pair_count, rows, cols = kept.shape
    smem = pl.BlockSpec(memory_space=pltpu.SMEM)
    vmem = pl.BlockSpec(memory_space=pltpu.VMEM)
    return pl.pallas_call(
        combine_kernel,
        in_specs=[smem, vmem, vmem, vmem],
        out_specs=vmem,
        out_shape=jax.ShapeDtypeStruct((16, pair_count * rows // 16, cols), jnp.float32),
        compiler_params=params(),
    )(partner, kept, same, other)


def turn(count, step):
    return [(i, (i + step) % count) for i in range(count)]


def mirror_pairs(other):
    pairs = []
    for r in range(16):
        for c in range(32):
            side = 1 - c % 2 if other else c % 2
            pairs.append((r * 32 + c, (c // 2) * 32 + 2 * r + side))
    return pairs


def on_device(amplitudes, factors, amp_mask, out_mask, partner):
    pair_count, amp_rows, amp_cols = amplitudes.shape
    batch_count, block_rows, full_width = factors.shape
    ring = 6
    first, second = prepare_call(amp_mask, amplitudes, factors, ring, 8)
    near = lax.all_to_all(second, "y", split_axis=0, concat_axis=0)
    units = lax.all_gather(gate_call(lax.all_gather(first, "zh", axis=0), near), "y", axis=0)

    back = lax.ppermute(near, "zh", turn(4, 1))
    ahead = lax.ppermute(near, "zh", turn(4, -1))
    left = lax.ppermute(back[:4], "zh", turn(4, 1))
    right = lax.ppermute(ahead[4:], "zh", turn(4, -1))

    early = early_call(factors, (near, back, ahead))
    late = late_call(factors, (left, right), early)
    core = lax.axis_index("core").reshape(1)
    send, inner = send_call(1 - core, factors, late, units)
    swapped = lax.ppermute(send, "core", turn(2, 1))
    keep = keep_call(core, inner, units)
    partial = (keep + swapped.astype(jnp.float32)).astype(jnp.bfloat16)
    pieces = lax.all_to_all(partial, ("zl", "x"), split_axis=0, concat_axis=0)
    kept, same, other = reduce_call(out_mask, pieces)
    same = lax.ppermute(same, ALL, mirror_pairs(False))
    other = lax.ppermute(other, ALL, mirror_pairs(True))
    rows = lax.all_to_all(combine_call(partner, kept, same, other), ROW, split_axis=0, concat_axis=0)
    rows = rows.reshape(16, pair_count, 4, 128).transpose(1, 2, 0, 3)
    return rows.reshape(pair_count, 4, full_width)


def solution(mesh):
    fine = Mesh(mesh.devices.reshape(2, 4, 2, 4, 8), ALL)
    return jax.shard_map(
        on_device,
        mesh=fine,
        in_specs=(P(None, COL, ROW), P(None, COL, None), P(), P(), P()),
        out_specs=P(None, COL + ROW, None),
        check_vma=False,
    )
```

```python
import jax
import jax.numpy as jnp
from jax import lax
from jax.experimental import pallas as pl
from jax.experimental.pallas import tpu as pltpu
from jax.sharding import Mesh, PartitionSpec as P

ROW = ("zl", "x", "core")
COL = ("zh", "y")
ALL = ROW + COL
MIB = 1024 * 1024


def params(mib=16):
    return pltpu.CompilerParams(vmem_limit_bytes=mib * MIB)


def place(names):
    at = lax.axis_index(names[0])
    for name in names[1:]:
        at = at * lax.axis_size(name) + lax.axis_index(name)
    return at


def prepare_kernel(mask_ref, amps_ref, factor_ref, first_ref, second_ref, copy_sem):
    batch_count, ring = factor_ref.shape[0], second_ref.shape[1]
    r = place(ROW)
    cols = amps_ref.shape[2]
    block = factor_ref.at[:, :, pl.ds(pl.multiple_of(r * cols, cols), cols)]
    copy = pltpu.make_async_copy(block, first_ref.at[:batch_count], copy_sem)
    copy.start()
    weight = mask_ref[place(COL) // 2, r].astype(jnp.float32).astype(jnp.bfloat16)
    masked = amps_ref[:ring] * weight
    for k in range(second_ref.shape[0]):
        second_ref[k] = masked
    first_ref[batch_count:] = amps_ref[ring:] * weight
    copy.wait()


def prepare_call(mask, amplitudes, factors, ring, copies):
    pair_count, rows, cols = amplitudes.shape
    flat = factors.shape[0] + pair_count - ring
    vmem = pl.BlockSpec(memory_space=pltpu.VMEM)
    return pl.pallas_call(
        prepare_kernel,
        in_specs=[pl.BlockSpec(memory_space=pltpu.SMEM), vmem, pl.BlockSpec(memory_space=pltpu.HBM)],
        out_specs=[vmem, vmem],
        out_shape=[
            jax.ShapeDtypeStruct((flat, rows, cols), jnp.bfloat16),
            jax.ShapeDtypeStruct((copies, ring, rows, cols), jnp.bfloat16),
        ],
        scratch_shapes=[pltpu.SemaphoreType.DMA],
        compiler_params=params(60),
    )(mask, amplitudes, factors)


def gate_kernel(held_ref, other_ref, out_ref):
    pass


def gate_call(held, other):
    anywhere = pl.BlockSpec(memory_space=pl.ANY)
    return pl.pallas_call(
        gate_kernel,
        in_specs=[anywhere, anywhere],
        out_specs=anywhere,
        out_shape=jax.ShapeDtypeStruct(held.shape, held.dtype),
        input_output_aliases={0: 0},
        compiler_params=params(),
    )(held, other)


def spread_product(product, out_ref, first, batch_count, block_rows):
    cols = out_ref.shape[0] // batch_count
    for pair in range(product.shape[1] // cols // 2):
        for q in range(batch_count):
            rows = product[q * block_rows : (q + 1) * block_rows, 2 * pair * cols : 2 * (pair + 1) * cols]
            block = jnp.concatenate([rows[:, :cols], rows[:, cols:]], axis=0)
            at = first + 2 * pair * block_rows
            out_ref[q * cols : (q + 1) * cols, at : at + 2 * block_rows] = block.T.astype(jnp.bfloat16)


def ring_term(own_ref, blocks, move):
    batch_count, block_rows, width = own_ref.shape
    group = width // 4
    at = pl.multiple_of(lax.rem(lax.axis_index("zh") + move, 4) * group, group)
    own = own_ref[:, :, pl.ds(at, group)].reshape(batch_count * block_rows, group)
    lanes = [
        jnp.concatenate([ref[k, p] for ref in blocks for k in range(ref.shape[0])], axis=0)
        for p in range(blocks[0].shape[1])
    ]
    return jnp.dot(own, jnp.concatenate(lanes, axis=1), preferred_element_type=jnp.float32)


def early_kernel(own_ref, near_ref, back_ref, ahead_ref, out_ref):
    product = ring_term(own_ref, [near_ref], 0)
    product = product + ring_term(own_ref, [back_ref], 3)
    out_ref[...] = product + ring_term(own_ref, [ahead_ref], 1)


def early_call(own, parts):
    batch_count, block_rows, width = own.shape
    pair_count, rows, cols = parts[0].shape[1:]
    return pl.pallas_call(
        early_kernel,
        grid=(pair_count // 2,),
        in_specs=[pl.BlockSpec(memory_space=pltpu.VMEM)]
        + [pl.BlockSpec((part.shape[0], 2, rows, cols), lambda i: (0, i, 0, 0)) for part in parts],
        out_specs=pl.BlockSpec((batch_count * block_rows, 2 * cols), lambda i: (0, i)),
        out_shape=jax.ShapeDtypeStruct((batch_count * block_rows, pair_count * cols), jnp.float32),
        compiler_params=params(),
    )(own, *parts)


def late_kernel(own_ref, left_ref, right_ref, early_ref, out_ref):
    batch_count, block_rows, width = own_ref.shape
    product = early_ref[...] + ring_term(own_ref, [left_ref, right_ref], 2)
    spread_product(product, out_ref, 0, batch_count, block_rows)


def late_call(own, parts, early):
    batch_count, block_rows, width = own.shape
    pair_count, rows, cols = parts[0].shape[1:]
    vmem = pl.BlockSpec(memory_space=pltpu.VMEM)
    return pl.pallas_call(
        late_kernel,
        in_specs=[vmem] * 4,
        out_specs=vmem,
        out_shape=jax.ShapeDtypeStruct((batch_count * cols, pair_count * block_rows), jnp.bfloat16),
        compiler_params=params(),
    )(own, *parts, early)


def ladder_term(inner_ref, low_ref, high_ref, out_ref):
    y_count, z_count, batch_count, rows, cols = low_ref.shape
    blocks = [(ref, z) for z in range(z_count) for ref in (low_ref, high_ref)]
    lanes = [
        jnp.concatenate([ref[y, z, q] for ref, z in blocks for y in range(y_count)], axis=0)
        for q in range(batch_count)
    ]
    factor = jnp.concatenate(lanes, axis=1)
    product = jnp.dot(factor, inner_ref[...], preferred_element_type=jnp.float32).astype(out_ref.dtype)
    height = y_count * rows
    for k in range(len(blocks)):
        out_ref[k] = product[k * height : (k + 1) * height]


def send_kernel(side_ref, own_ref, ring_ref, *refs):
    amps_refs, (low_ref, high_ref, out_ref, inner_ref) = refs[:-4], refs[-4:]
    batch_count, block_rows, width = own_ref.shape
    ring = ring_ref.shape[1]

    @pl.when(pl.program_id(0) == 0)
    def _():
        inner_ref[:, :ring] = ring_ref[...]
        own = own_ref[...].reshape(batch_count * block_rows, width)
        lanes = [
            jnp.concatenate([ref[y, z, 0] for z in range(ref.shape[1]) for y in range(ref.shape[0])], axis=0)
            for ref in amps_refs
        ]
        product = jnp.dot(own, jnp.concatenate(lanes, axis=1), preferred_element_type=jnp.float32)
        spread_product(product, inner_ref, ring, batch_count, block_rows)

    pl.when(pl.program_id(0) > 0)(lambda: ladder_term(inner_ref, low_ref, high_ref, out_ref))


ZSTEP = 2


def send_call(side, own, ring_inner, units):
    depth, ring_width = ring_inner.shape
    batch_count, block_rows, width = own.shape
    y_count, z_count, unit_count, rows, cols = units.shape
    flat = unit_count - batch_count
    inner_width = ring_width + flat * block_rows
    quarter = (y_count // 4, ZSTEP, batch_count, rows, cols)
    blocks = 2 * ZSTEP

    def amps_spec(k):
        return pl.BlockSpec((y_count, z_count, 1, rows, cols), lambda i, side: (0, 0, batch_count + k, 0, 0))

    return pl.pallas_call(
        send_kernel,
        grid_spec=pltpu.PrefetchScalarGridSpec(
            num_scalar_prefetch=1,
            grid=(z_count // ZSTEP + 1,),
            in_specs=[pl.BlockSpec(memory_space=pltpu.VMEM)] * 2
            + [amps_spec(k) for k in range(flat)]
            + [
                pl.BlockSpec(quarter, lambda i, side: (side[0], jnp.maximum(i - 1, 0), 0, 0, 0)),
                pl.BlockSpec(quarter, lambda i, side: (side[0] + 2, jnp.maximum(i - 1, 0), 0, 0, 0)),
            ],
            out_specs=[
                pl.BlockSpec((blocks, 2 * rows, inner_width), lambda i, side: (jnp.maximum(i - 1, 0), 0, 0)),
                pl.BlockSpec((depth, inner_width), lambda i, side: (0, 0)),
            ],
        ),
        out_shape=[
            jax.ShapeDtypeStruct((8, 2 * rows, inner_width), jnp.bfloat16),
            jax.ShapeDtypeStruct((depth, inner_width), jnp.bfloat16),
        ],
        compiler_params=params(48),
    )(side, own, ring_inner, *[units] * (flat + 2))


def keep_kernel(side_ref, inner_ref, low_ref, high_ref, out_ref):
    ladder_term(inner_ref, low_ref, high_ref, out_ref)


def keep_call(side, inner, units):
    depth, inner_width = inner.shape
    y_count, z_count, unit_count, rows, cols = units.shape
    quarter = (y_count // 4, ZSTEP, depth // cols, rows, cols)
    return pl.pallas_call(
        keep_kernel,
        grid_spec=pltpu.PrefetchScalarGridSpec(
            num_scalar_prefetch=1,
            grid=(z_count // ZSTEP,),
            in_specs=[
                pl.BlockSpec(memory_space=pltpu.VMEM),
                pl.BlockSpec(quarter, lambda i, side: (side[0], i, 0, 0, 0)),
                pl.BlockSpec(quarter, lambda i, side: (side[0] + 2, i, 0, 0, 0)),
            ],
            out_specs=pl.BlockSpec((2 * ZSTEP, 2 * rows, inner_width), lambda i, side: (i, 0, 0)),
        ),
        out_shape=jax.ShapeDtypeStruct((8, 2 * rows, inner_width), jnp.float32),
        compiler_params=params(48),
    )(side, inner, units, units)


def reduce_kernel(mask_ref, part_ref, kept_ref, same_ref, other_ref):
    c = place(COL)
    weight = mask_ref[c // 2, place(ROW)].astype(jnp.float32)
    side = lax.rem(c, 2)
    half = kept_ref.shape[1]
    total = part_ref[0].astype(jnp.float32)
    for k in range(1, part_ref.shape[0]):
        total = total + part_ref[k].astype(jnp.float32)
    total = total * weight
    straight = total.T
    kept_ref[0], kept_ref[1] = straight[:half], straight[half:]
    turned = total.astype(jnp.bfloat16)
    low, high = turned[:half], turned[half:]
    same_ref[0] = jnp.where(side == 0, low, high)
    other_ref[0] = jnp.where(side == 0, high, low)


def reduce_call(mask, pieces, rows):
    sources, cols, inner_width = pieces.shape
    pair_count = inner_width // rows
    half_spec = pl.BlockSpec((1, rows, cols), lambda i: (i, 0, 0))
    return pl.pallas_call(
        reduce_kernel,
        grid=(pair_count // 2,),
        in_specs=[
            pl.BlockSpec(memory_space=pltpu.SMEM),
            pl.BlockSpec((sources, cols, 2 * rows), lambda i: (0, 0, i)),
        ],
        out_specs=[pl.BlockSpec((2, rows, cols), lambda i: (i, 0, 0)), half_spec, half_spec],
        out_shape=[
            jax.ShapeDtypeStruct((pair_count, rows, cols), jnp.float32),
            jax.ShapeDtypeStruct((pair_count // 2, rows, cols), jnp.bfloat16),
            jax.ShapeDtypeStruct((pair_count // 2, rows, cols), jnp.bfloat16),
        ],
        compiler_params=params(),
    )(mask, pieces)


def combine_kernel(partner_ref, kept_ref, same_ref, other_ref, out_ref):
    side = lax.rem(place(COL), 2)
    pair_count, rows, cols = kept_ref.shape
    half = cols // 2
    for p in range(pair_count):
        mate = partner_ref[p]
        odd = lax.rem(mate, 2) == 1
        same = same_ref[mate // 2].astype(jnp.float32)
        other = other_ref[mate // 2].astype(jnp.float32)
        same = jnp.where(odd, same[:, half:], same[:, :half])
        other = jnp.where(odd, other[:, half:], other[:, :half])
        first = jnp.where(side == 0, same, other)
        second = jnp.where(side == 0, other, same)
        total = kept_ref[p] + jnp.concatenate([first, second], axis=1)
        for k in range(16):
            out_ref[k, p * 4 : (p + 1) * 4, :] = total[k * 4 : (k + 1) * 4]


def combine_call(partner, kept, same, other):
    pair_count, rows, cols = kept.shape
    smem = pl.BlockSpec(memory_space=pltpu.SMEM)
    vmem = pl.BlockSpec(memory_space=pltpu.VMEM)
    return pl.pallas_call(
        combine_kernel,
        in_specs=[smem, vmem, vmem, vmem],
        out_specs=vmem,
        out_shape=jax.ShapeDtypeStruct((16, pair_count * rows // 16, cols), jnp.float32),
        compiler_params=params(),
    )(partner, kept, same, other)


def turn(count, step):
    return [(i, (i + step) % count) for i in range(count)]


def mirror_pairs(other):
    pairs = []
    for r in range(16):
        for c in range(32):
            side = 1 - c % 2 if other else c % 2
            pairs.append((r * 32 + c, (c // 2) * 32 + 2 * r + side))
    return pairs


def on_device(amplitudes, factors, amp_mask, out_mask, partner):
    pair_count, amp_rows, amp_cols = amplitudes.shape
    batch_count, block_rows, full_width = factors.shape
    ring = 6
    first, second = prepare_call(amp_mask, amplitudes, factors, ring, 8)
    near = lax.all_to_all(second, "y", split_axis=0, concat_axis=0)
    units = lax.all_gather(gate_call(lax.all_gather(first, "zh", axis=0), near), "y", axis=0)

    back = lax.ppermute(near, "zh", turn(4, 1))
    ahead = lax.ppermute(near, "zh", turn(4, -1))
    left = lax.ppermute(back[:4], "zh", turn(4, 1))
    right = lax.ppermute(ahead[4:], "zh", turn(4, -1))

    early = early_call(factors, (near, back, ahead))
    late = late_call(factors, (left, right), early)
    core = lax.axis_index("core").reshape(1)
    send, inner = send_call(1 - core, factors, late, units)
    swapped = lax.ppermute(send, "core", turn(2, 1))
    keep = keep_call(core, inner, units)
    partial = (keep + swapped.astype(jnp.float32)).astype(jnp.bfloat16)
    pieces = lax.all_to_all(partial, ("zl", "x"), split_axis=0, concat_axis=0)
    kept, same, other = reduce_call(out_mask, pieces, block_rows)
    same = lax.ppermute(same, ALL, mirror_pairs(False))
    other = lax.ppermute(other, ALL, mirror_pairs(True))
    rows = lax.all_to_all(combine_call(partner, kept, same, other), ROW, split_axis=0, concat_axis=0)
    rows = rows.reshape(16, pair_count, 4, 128).transpose(1, 2, 0, 3)
    return rows.reshape(pair_count, 4, full_width)


def solution(mesh):
    fine = Mesh(mesh.devices.reshape(2, 4, 2, 4, 8), ALL)
    return jax.shard_map(
        on_device,
        mesh=fine,
        in_specs=(P(None, COL, ROW), P(None, COL, None), P(), P(), P()),
        out_specs=P(None, COL + ROW, None),
        check_vma=False,
    )
```

```python
import functools

import jax
import jax.numpy as jnp
from jax import lax
from jax.experimental import pallas as pl
from jax.experimental.pallas import tpu as pltpu
from jax.sharding import Mesh, PartitionSpec as P

ROW = ("zl", "x", "core")
COL = ("zh", "y")
ALL = ROW + COL
MIB = 1024 * 1024


def params(mib=16):
    return pltpu.CompilerParams(vmem_limit_bytes=mib * MIB)


def place(names):
    at = lax.axis_index(names[0])
    for name in names[1:]:
        at = at * lax.axis_size(name) + lax.axis_index(name)
    return at


def prepare_kernel(mask_ref, amps_ref, factor_ref, first_ref, second_ref, masked_ref, slice_ref, sems):
    batch_count, (copies, ring) = factor_ref.shape[0], second_ref.shape[:2]
    r = place(ROW)
    cols = amps_ref.shape[2]
    load = pltpu.make_async_copy(amps_ref, masked_ref, sems.at[0])
    load.start()
    block = factor_ref.at[:, :, pl.ds(pl.multiple_of(r * cols, cols), cols)]
    fetch = pltpu.make_async_copy(block, slice_ref, sems.at[1])
    fetch.start()
    weight = mask_ref[place(COL) // 2, r].astype(jnp.float32).astype(jnp.bfloat16)
    load.wait()
    masked_ref[...] = masked_ref[...] * weight
    stores = [pltpu.make_async_copy(masked_ref.at[ring:], first_ref.at[batch_count:], sems.at[2])]
    for k in range(copies):
        stores.append(pltpu.make_async_copy(masked_ref.at[:ring], second_ref.at[k], sems.at[4 + k]))
    for store in stores:
        store.start()
    fetch.wait()
    stores.append(pltpu.make_async_copy(slice_ref, first_ref.at[:batch_count], sems.at[3]))
    stores[-1].start()
    for store in stores:
        store.wait()


def prepare_call(mask, amplitudes, factors, ring, copies):
    pair_count, rows, cols = amplitudes.shape
    flat = factors.shape[0] + pair_count - ring
    hbm = pl.BlockSpec(memory_space=pltpu.HBM)
    return pl.pallas_call(
        prepare_kernel,
        in_specs=[pl.BlockSpec(memory_space=pltpu.SMEM), hbm, hbm],
        out_specs=[hbm, hbm],
        out_shape=[
            jax.ShapeDtypeStruct((flat, rows, cols), jnp.bfloat16),
            jax.ShapeDtypeStruct((copies, ring, rows, cols), jnp.bfloat16),
        ],
        scratch_shapes=[
            pltpu.VMEM(amplitudes.shape, jnp.bfloat16),
            pltpu.VMEM((factors.shape[0], rows, cols), jnp.bfloat16),
            pltpu.SemaphoreType.DMA((4 + copies,)),
        ],
        compiler_params=params(60),
    )(mask, amplitudes, factors)


def gate_kernel(held_ref, other_ref, out_ref):
    pass


def gate_call(held, other):
    anywhere = pl.BlockSpec(memory_space=pl.ANY)
    return pl.pallas_call(
        gate_kernel,
        in_specs=[anywhere, anywhere],
        out_specs=anywhere,
        out_shape=jax.ShapeDtypeStruct(held.shape, held.dtype),
        input_output_aliases={0: 0},
        compiler_params=params(),
    )(held, other)


def spread_product(product, out_ref, first, batch_count, block_rows):
    cols = out_ref.shape[0] // batch_count
    for pair in range(product.shape[1] // cols // 2):
        for q in range(batch_count):
            rows = product[q * block_rows : (q + 1) * block_rows, 2 * pair * cols : 2 * (pair + 1) * cols]
            block = jnp.concatenate([rows[:, :cols], rows[:, cols:]], axis=0)
            at = first + 2 * pair * block_rows
            out_ref[q * cols : (q + 1) * cols, at : at + 2 * block_rows] = block.T.astype(jnp.bfloat16)


def ring_term(own_ref, blocks, move):
    batch_count, block_rows, width = own_ref.shape
    group = width // 4
    at = pl.multiple_of(lax.rem(lax.axis_index("zh") + move, 4) * group, group)
    own = own_ref[:, :, pl.ds(at, group)].reshape(batch_count * block_rows, group)
    lanes = [
        jnp.concatenate([ref[k, p] for ref in blocks for k in range(ref.shape[0])], axis=0)
        for p in range(blocks[0].shape[1])
    ]
    return jnp.dot(own, jnp.concatenate(lanes, axis=1), preferred_element_type=jnp.float32)


def early_kernel(own_ref, near_ref, back_ref, ahead_ref, out_ref):
    product = ring_term(own_ref, [near_ref], 0)
    product = product + ring_term(own_ref, [back_ref], 3)
    out_ref[...] = product + ring_term(own_ref, [ahead_ref], 1)


def early_call(own, parts):
    batch_count, block_rows, width = own.shape
    pair_count, rows, cols = parts[0].shape[1:]
    return pl.pallas_call(
        early_kernel,
        grid=(pair_count // 2,),
        in_specs=[pl.BlockSpec(memory_space=pltpu.VMEM)]
        + [pl.BlockSpec((part.shape[0], 2, rows, cols), lambda i: (0, i, 0, 0)) for part in parts],
        out_specs=pl.BlockSpec((batch_count * block_rows, 2 * cols), lambda i: (0, i)),
        out_shape=jax.ShapeDtypeStruct((batch_count * block_rows, pair_count * cols), jnp.float32),
        compiler_params=params(),
    )(own, *parts)


def late_kernel(own_ref, left_ref, right_ref, early_ref, out_ref):
    batch_count, block_rows, width = own_ref.shape
    product = early_ref[...] + ring_term(own_ref, [left_ref, right_ref], 2)
    spread_product(product, out_ref, 0, batch_count, block_rows)


def late_call(own, parts, early):
    batch_count, block_rows, width = own.shape
    pair_count, rows, cols = parts[0].shape[1:]
    vmem = pl.BlockSpec(memory_space=pltpu.VMEM)
    return pl.pallas_call(
        late_kernel,
        in_specs=[vmem] * 4,
        out_specs=vmem,
        out_shape=jax.ShapeDtypeStruct((batch_count * cols, pair_count * block_rows), jnp.bfloat16),
        compiler_params=params(),
    )(own, *parts, early)


def flat_kernel(own_ref, units_ref, out_ref, amps_ref, sems):
    batch_count, block_rows, width = own_ref.shape
    y_count, z_count, pairs, rows, cols = amps_ref.shape
    loads = []
    for p in range(pairs):
        block = units_ref.at[:, :, batch_count + p]
        loads.append(pltpu.make_async_copy(block, amps_ref.at[:, :, p], sems.at[p]))
        loads[p].start()
    lanes = []
    for p in range(pairs):
        loads[p].wait()
        lanes.append(jnp.concatenate([amps_ref[y, z, p] for z in range(z_count) for y in range(y_count)], axis=0))
    own = own_ref[...].reshape(batch_count * block_rows, width)
    product = jnp.dot(own, jnp.concatenate(lanes, axis=1), preferred_element_type=jnp.float32)
    spread_product(product, out_ref, 0, batch_count, block_rows)


def flat_call(own, units):
    batch_count, block_rows, width = own.shape
    y_count, z_count, unit_count, rows, cols = units.shape
    pairs = unit_count - batch_count
    vmem = pl.BlockSpec(memory_space=pltpu.VMEM)
    return pl.pallas_call(
        flat_kernel,
        in_specs=[vmem, pl.BlockSpec(memory_space=pltpu.HBM)],
        out_specs=vmem,
        out_shape=jax.ShapeDtypeStruct((batch_count * cols, pairs * block_rows), jnp.bfloat16),
        scratch_shapes=[
            pltpu.VMEM((y_count, z_count, pairs, rows, cols), jnp.bfloat16),
            pltpu.SemaphoreType.DMA((pairs,)),
        ],
        compiler_params=params(48),
    )(own, units)


def ladder_kernel(flip, ring_ref, flat_ref, units_ref, out_ref, block_ref, sems):
    y_count, z_count, batch_count, rows, cols = block_ref.shape
    side = lax.rem(lax.axis_index("core") + flip, 2)
    pair, step = y_count // 2, z_count // 2
    loads = []
    for k in range(2):
        for half in range(2):
            source = units_ref.at[pl.ds((side + 2 * half) * pair, pair), pl.ds(k * step, step), pl.ds(0, batch_count)]
            target = block_ref.at[pl.ds(half * pair, pair), pl.ds(k * step, step)]
            loads.append(pltpu.make_async_copy(source, target, sems.at[2 * k + half]))
            loads[-1].start()
    inner = jnp.concatenate([ring_ref[...], flat_ref[...]], axis=1)
    height = pair * rows
    for k in range(2):
        loads[2 * k].wait()
        loads[2 * k + 1].wait()
        places = [(z, y) for z in range(k * step, (k + 1) * step) for y in range(y_count)]
        lanes = [jnp.concatenate([block_ref[y, z, q] for z, y in places], axis=0) for q in range(batch_count)]
        factor = jnp.concatenate(lanes, axis=1)
        product = jnp.dot(factor, inner, preferred_element_type=jnp.float32).astype(out_ref.dtype)
        for m in range(2 * step):
            out_ref[2 * step * k + m] = product[m * height : (m + 1) * height]


def ladder_call(flip, ring, flat, units, kind):
    depth, width = ring.shape[0], ring.shape[1] + flat.shape[1]
    y_count, z_count, unit_count, rows, cols = units.shape
    batch_count = depth // cols
    vmem = pl.BlockSpec(memory_space=pltpu.VMEM)
    return pl.pallas_call(
        functools.partial(ladder_kernel, flip),
        in_specs=[vmem, vmem, pl.BlockSpec(memory_space=pltpu.HBM)],
        out_specs=vmem,
        out_shape=jax.ShapeDtypeStruct((2 * z_count, y_count // 4 * rows, width), kind),
        scratch_shapes=[
            pltpu.VMEM((y_count // 2, z_count, batch_count, rows, cols), jnp.bfloat16),
            pltpu.SemaphoreType.DMA((4,)),
        ],
        compiler_params=params(48),
    )(ring, flat, units)


def reduce_kernel(mask_ref, part_ref, kept_ref, same_ref, other_ref):
    c = place(COL)
    weight = mask_ref[c // 2, place(ROW)].astype(jnp.float32)
    side = lax.rem(c, 2)
    half = kept_ref.shape[1]
    total = part_ref[0].astype(jnp.float32)
    for k in range(1, part_ref.shape[0]):
        total = total + part_ref[k].astype(jnp.float32)
    total = total * weight
    straight = total.T
    kept_ref[0], kept_ref[1] = straight[:half], straight[half:]
    turned = total.astype(jnp.bfloat16)
    low, high = turned[:half], turned[half:]
    same_ref[0] = jnp.where(side == 0, low, high)
    other_ref[0] = jnp.where(side == 0, high, low)


def reduce_call(mask, pieces, rows):
    sources, cols, inner_width = pieces.shape
    pair_count = inner_width // rows
    half_spec = pl.BlockSpec((1, rows, cols), lambda i: (i, 0, 0))
    return pl.pallas_call(
        reduce_kernel,
        grid=(pair_count // 2,),
        in_specs=[
            pl.BlockSpec(memory_space=pltpu.SMEM),
            pl.BlockSpec((sources, cols, 2 * rows), lambda i: (0, 0, i)),
        ],
        out_specs=[pl.BlockSpec((2, rows, cols), lambda i: (i, 0, 0)), half_spec, half_spec],
        out_shape=[
            jax.ShapeDtypeStruct((pair_count, rows, cols), jnp.float32),
            jax.ShapeDtypeStruct((pair_count // 2, rows, cols), jnp.bfloat16),
            jax.ShapeDtypeStruct((pair_count // 2, rows, cols), jnp.bfloat16),
        ],
        compiler_params=params(),
    )(mask, pieces)


def combine_kernel(partner_ref, kept_ref, same_ref, other_ref, out_ref):
    side = lax.rem(place(COL), 2)
    pair_count, rows, cols = kept_ref.shape
    half = cols // 2
    for p in range(pair_count):
        mate = partner_ref[p]
        odd = lax.rem(mate, 2) == 1
        same = same_ref[mate // 2].astype(jnp.float32)
        other = other_ref[mate // 2].astype(jnp.float32)
        same = jnp.where(odd, same[:, half:], same[:, :half])
        other = jnp.where(odd, other[:, half:], other[:, :half])
        first = jnp.where(side == 0, same, other)
        second = jnp.where(side == 0, other, same)
        total = kept_ref[p] + jnp.concatenate([first, second], axis=1)
        for k in range(16):
            out_ref[k, p * 4 : (p + 1) * 4, :] = total[k * 4 : (k + 1) * 4]


def combine_call(partner, kept, same, other):
    pair_count, rows, cols = kept.shape
    smem = pl.BlockSpec(memory_space=pltpu.SMEM)
    vmem = pl.BlockSpec(memory_space=pltpu.VMEM)
    return pl.pallas_call(
        combine_kernel,
        in_specs=[smem, vmem, vmem, vmem],
        out_specs=vmem,
        out_shape=jax.ShapeDtypeStruct((16, pair_count * rows // 16, cols), jnp.float32),
        compiler_params=params(),
    )(partner, kept, same, other)


def turn(count, step):
    return [(i, (i + step) % count) for i in range(count)]


def mirror_pairs(other):
    pairs = []
    for r in range(16):
        for c in range(32):
            side = 1 - c % 2 if other else c % 2
            pairs.append((r * 32 + c, (c // 2) * 32 + 2 * r + side))
    return pairs


def on_device(amplitudes, factors, amp_mask, out_mask, partner):
    pair_count, amp_rows, amp_cols = amplitudes.shape
    batch_count, block_rows, full_width = factors.shape
    ring = 6
    first, second = prepare_call(amp_mask, amplitudes, factors, ring, 8)
    near = lax.all_to_all(second, "y", split_axis=0, concat_axis=0)
    units = lax.all_gather(gate_call(lax.all_gather(first, "zh", axis=0), near), "y", axis=0)

    back = lax.ppermute(near, "zh", turn(4, 1))
    ahead = lax.ppermute(near, "zh", turn(4, -1))
    left = lax.ppermute(back[:4], "zh", turn(4, 1))
    right = lax.ppermute(ahead[4:], "zh", turn(4, -1))

    early = early_call(factors, (near, back, ahead))
    late = late_call(factors, (left, right), early)
    flat = flat_call(factors, units)
    swapped = lax.ppermute(ladder_call(1, late, flat, units, jnp.bfloat16), "core", turn(2, 1))
    keep = ladder_call(0, late, flat, units, jnp.float32)
    partial = (keep + swapped.astype(jnp.float32)).astype(jnp.bfloat16)
    pieces = lax.all_to_all(partial, ("zl", "x"), split_axis=0, concat_axis=0)
    kept, same, other = reduce_call(out_mask, pieces, block_rows)
    same = lax.ppermute(same, ALL, mirror_pairs(False))
    other = lax.ppermute(other, ALL, mirror_pairs(True))
    rows = lax.all_to_all(combine_call(partner, kept, same, other), ROW, split_axis=0, concat_axis=0)
    rows = rows.reshape(16, pair_count, 4, 128).transpose(1, 2, 0, 3)
    return rows.reshape(pair_count, 4, full_width)


def solution(mesh):
    fine = Mesh(mesh.devices.reshape(2, 4, 2, 4, 8), ALL)
    return jax.shard_map(
        on_device,
        mesh=fine,
        in_specs=(P(None, COL, ROW), P(None, COL, None), P(), P(), P()),
        out_specs=P(None, COL + ROW, None),
        check_vma=False,
    )
```

```python
import functools

import jax
import jax.numpy as jnp
from jax import lax
from jax.experimental import pallas as pl
from jax.experimental.pallas import tpu as pltpu
from jax.sharding import Mesh, PartitionSpec as P

ROW = ("zl", "x", "core")
COL = ("zh", "y")
ALL = ROW + COL
MIB = 1024 * 1024


def params(mib=16):
    return pltpu.CompilerParams(vmem_limit_bytes=mib * MIB)


def place(names):
    at = lax.axis_index(names[0])
    for name in names[1:]:
        at = at * lax.axis_size(name) + lax.axis_index(name)
    return at


def prepare_kernel(mask_ref, amps_ref, factor_ref, first_ref, second_ref, masked_ref, slice_ref, order_ref, sems):
    batch_count, (copies, ring) = factor_ref.shape[0], second_ref.shape[:2]
    r = place(ROW)
    cols = amps_ref.shape[2]
    load = pltpu.make_async_copy(amps_ref, masked_ref, sems.at[0])
    load.start()
    block = factor_ref.at[:, :, pl.ds(pl.multiple_of(r * cols, cols), cols)]
    fetch = pltpu.make_async_copy(block, slice_ref, sems.at[1])
    fetch.start()
    weight = mask_ref[place(COL) // 2, r].astype(jnp.float32).astype(jnp.bfloat16)
    load.wait()
    masked_ref[...] = masked_ref[...] * weight
    stores = [pltpu.make_async_copy(masked_ref.at[ring:], first_ref.at[batch_count:], sems.at[2])]
    for k in range(copies):
        stores.append(pltpu.make_async_copy(masked_ref.at[:ring], second_ref.at[k], sems.at[4 + k]))
    for store in stores:
        store.start()
    fetch.wait()
    rows = slice_ref[...].astype(jnp.float32)
    half = rows.shape[1] // 2
    for k in range(half // 4):
        for core in range(2):
            at = core * half + k * 4
            order_ref[:, at : at + 4, :] = rows[:, (2 * k + core) * 4 : (2 * k + core + 1) * 4, :]
    slice_ref[...] = order_ref[...].astype(jnp.bfloat16)
    stores.append(pltpu.make_async_copy(slice_ref, first_ref.at[:batch_count], sems.at[3]))
    stores[-1].start()
    for store in stores:
        store.wait()


def prepare_call(mask, amplitudes, factors, ring, copies):
    pair_count, rows, cols = amplitudes.shape
    flat = factors.shape[0] + pair_count - ring
    hbm = pl.BlockSpec(memory_space=pltpu.HBM)
    return pl.pallas_call(
        prepare_kernel,
        in_specs=[pl.BlockSpec(memory_space=pltpu.SMEM), hbm, hbm],
        out_specs=[hbm, hbm],
        out_shape=[
            jax.ShapeDtypeStruct((flat, rows, cols), jnp.bfloat16),
            jax.ShapeDtypeStruct((copies, ring, rows, cols), jnp.bfloat16),
        ],
        scratch_shapes=[
            pltpu.VMEM(amplitudes.shape, jnp.bfloat16),
            pltpu.VMEM((factors.shape[0], rows, cols), jnp.bfloat16),
            pltpu.VMEM((factors.shape[0], rows, cols), jnp.float32),
            pltpu.SemaphoreType.DMA((4 + copies,)),
        ],
        compiler_params=params(60),
    )(mask, amplitudes, factors)


def gate_kernel(held_ref, other_ref, out_ref):
    pass


def gate_call(held, other):
    anywhere = pl.BlockSpec(memory_space=pl.ANY)
    return pl.pallas_call(
        gate_kernel,
        in_specs=[anywhere, anywhere],
        out_specs=anywhere,
        out_shape=jax.ShapeDtypeStruct(held.shape, held.dtype),
        input_output_aliases={0: 0},
        compiler_params=params(),
    )(held, other)


def spread_product(product, out_ref, first, batch_count, block_rows):
    cols = out_ref.shape[0] // batch_count
    for pair in range(product.shape[1] // cols // 2):
        for q in range(batch_count):
            rows = product[q * block_rows : (q + 1) * block_rows, 2 * pair * cols : 2 * (pair + 1) * cols]
            block = jnp.concatenate([rows[:, :cols], rows[:, cols:]], axis=0)
            at = first + 2 * pair * block_rows
            out_ref[q * cols : (q + 1) * cols, at : at + 2 * block_rows] = block.T.astype(jnp.bfloat16)


def ring_term(own_ref, blocks, move):
    batch_count, block_rows, width = own_ref.shape
    group = width // 4
    at = pl.multiple_of(lax.rem(lax.axis_index("zh") + move, 4) * group, group)
    own = own_ref[:, :, pl.ds(at, group)].reshape(batch_count * block_rows, group)
    lanes = [
        jnp.concatenate([ref[k, p] for ref in blocks for k in range(ref.shape[0])], axis=0)
        for p in range(blocks[0].shape[1])
    ]
    return jnp.dot(own, jnp.concatenate(lanes, axis=1), preferred_element_type=jnp.float32)


def early_kernel(own_ref, near_ref, back_ref, ahead_ref, out_ref):
    product = ring_term(own_ref, [near_ref], 0)
    product = product + ring_term(own_ref, [back_ref], 3)
    out_ref[...] = product + ring_term(own_ref, [ahead_ref], 1)


def early_call(own, parts):
    batch_count, block_rows, width = own.shape
    pair_count, rows, cols = parts[0].shape[1:]
    return pl.pallas_call(
        early_kernel,
        grid=(pair_count // 2,),
        in_specs=[pl.BlockSpec(memory_space=pltpu.VMEM)]
        + [pl.BlockSpec((part.shape[0], 2, rows, cols), lambda i: (0, i, 0, 0)) for part in parts],
        out_specs=pl.BlockSpec((batch_count * block_rows, 2 * cols), lambda i: (0, i)),
        out_shape=jax.ShapeDtypeStruct((batch_count * block_rows, pair_count * cols), jnp.float32),
        compiler_params=params(),
    )(own, *parts)


def late_kernel(own_ref, left_ref, right_ref, early_ref, out_ref):
    batch_count, block_rows, width = own_ref.shape
    product = early_ref[...] + ring_term(own_ref, [left_ref, right_ref], 2)
    spread_product(product, out_ref, 0, batch_count, block_rows)


def late_call(own, parts, early):
    batch_count, block_rows, width = own.shape
    pair_count, rows, cols = parts[0].shape[1:]
    vmem = pl.BlockSpec(memory_space=pltpu.VMEM)
    return pl.pallas_call(
        late_kernel,
        in_specs=[vmem] * 4,
        out_specs=vmem,
        out_shape=jax.ShapeDtypeStruct((batch_count * cols, pair_count * block_rows), jnp.bfloat16),
        compiler_params=params(),
    )(own, *parts, early)


def flat_kernel(own_ref, units_ref, out_ref, amps_ref, sems):
    batch_count, block_rows, width = own_ref.shape
    y_count, z_count, pairs, rows, cols = amps_ref.shape
    loads = []
    for p in range(pairs):
        block = units_ref.at[:, :, batch_count + p]
        loads.append(pltpu.make_async_copy(block, amps_ref.at[:, :, p], sems.at[p]))
        loads[p].start()
    lanes = []
    for p in range(pairs):
        loads[p].wait()
        lanes.append(jnp.concatenate([amps_ref[y, z, p] for z in range(z_count) for y in range(y_count)], axis=0))
    own = own_ref[...].reshape(batch_count * block_rows, width)
    product = jnp.dot(own, jnp.concatenate(lanes, axis=1), preferred_element_type=jnp.float32)
    spread_product(product, out_ref, 0, batch_count, block_rows)


def flat_call(own, units):
    batch_count, block_rows, width = own.shape
    y_count, z_count, unit_count, rows, cols = units.shape
    pairs = unit_count - batch_count
    vmem = pl.BlockSpec(memory_space=pltpu.VMEM)
    return pl.pallas_call(
        flat_kernel,
        in_specs=[vmem, pl.BlockSpec(memory_space=pltpu.HBM)],
        out_specs=vmem,
        out_shape=jax.ShapeDtypeStruct((batch_count * cols, pairs * block_rows), jnp.bfloat16),
        scratch_shapes=[
            pltpu.VMEM((y_count, z_count, pairs, rows, cols), jnp.bfloat16),
            pltpu.SemaphoreType.DMA((pairs,)),
        ],
        compiler_params=params(48),
    )(own, units)


def ladder_kernel(flip, ring_ref, flat_ref, units_ref, out_ref, block_ref, sems):
    y_count, z_count, batch_count, rows, cols = block_ref.shape
    side = lax.rem(lax.axis_index("core") + flip, 2)
    step = z_count // 2
    here = pl.ds(pl.multiple_of(side * rows, rows), rows)
    loads = []
    for k in range(2):
        span = pl.ds(k * step, step)
        source = units_ref.at[:, span, pl.ds(0, batch_count), here]
        loads.append(pltpu.make_async_copy(source, block_ref.at[:, span], sems.at[k]))
        loads[-1].start()
    inner = jnp.concatenate([ring_ref[...], flat_ref[...]], axis=1)
    height = step * y_count * rows
    for k in range(2):
        loads[k].wait()
        places = [(z, y) for z in range(k * step, (k + 1) * step) for y in range(y_count)]
        lanes = [jnp.concatenate([block_ref[y, z, q] for z, y in places], axis=0) for q in range(batch_count)]
        factor = jnp.concatenate(lanes, axis=1)
        product = jnp.dot(factor, inner, preferred_element_type=jnp.float32)
        out_ref[k * height : (k + 1) * height] = product.astype(out_ref.dtype)


def ladder_call(flip, ring, flat, units, kind):
    depth, width = ring.shape[0], ring.shape[1] + flat.shape[1]
    y_count, z_count, unit_count, rows, cols = units.shape
    vmem = pl.BlockSpec(memory_space=pltpu.VMEM)
    return pl.pallas_call(
        functools.partial(ladder_kernel, flip),
        in_specs=[vmem, vmem, pl.BlockSpec(memory_space=pltpu.HBM)],
        out_specs=vmem,
        out_shape=jax.ShapeDtypeStruct((y_count * z_count * rows // 2, width), kind),
        scratch_shapes=[
            pltpu.VMEM((y_count, z_count, depth // cols, rows // 2, cols), jnp.bfloat16),
            pltpu.SemaphoreType.DMA((2,)),
        ],
        compiler_params=params(48),
    )(ring, flat, units)


def swing(block, axis):
    half = block.shape[axis] // 2
    first = lax.slice_in_dim(block, 0, half, axis=axis)
    return jnp.concatenate([lax.slice_in_dim(block, half, 2 * half, axis=axis), first], axis=axis)


def gather_kernel(keep_ref, other_ref, out_ref):
    groups, height, cols = out_ref.shape
    total = keep_ref[...] + other_ref[...].astype(jnp.float32)
    tiles = total.reshape(height // 8, 2, groups // 2, 8, cols)
    top = lax.broadcasted_iota(jnp.int32, (height // 8, 8, cols), 1) < 4
    for k in range(groups // 2):
        first, second = tiles[:, 0, k], tiles[:, 1, k]
        even = jnp.where(top, first, swing(second, 1))
        odd = jnp.where(top, swing(first, 1), second)
        out_ref[2 * k] = even.reshape(height, cols).astype(jnp.bfloat16)
        out_ref[2 * k + 1] = odd.reshape(height, cols).astype(jnp.bfloat16)


def gather_call(keep, other, groups):
    height, width = keep.shape
    cols = 128
    return pl.pallas_call(
        gather_kernel,
        grid=(width // cols,),
        in_specs=[pl.BlockSpec((height, cols), lambda i: (0, i))] * 2,
        out_specs=pl.BlockSpec((groups, height // groups, cols), lambda i: (0, 0, i)),
        out_shape=jax.ShapeDtypeStruct((groups, height // groups, width), jnp.bfloat16),
        compiler_params=params(),
    )(keep, other)


def reduce_kernel(mask_ref, part_ref, direct_ref, mirror_ref, stage_ref):
    sources, height, width = part_ref.shape
    cols = direct_ref.shape[3]
    half = cols // 2
    row = place(COL) // 2
    for k in range(width // cols):
        span = slice(k * cols, (k + 1) * cols)
        total = part_ref[0, :, span].astype(jnp.float32)
        for m in range(1, sources):
            total = total + part_ref[m, :, span].astype(jnp.float32)
        tiles = [total[t * 8 : (t + 1) * 8] * mask_ref[row, t].astype(jnp.float32) for t in range(height // 8)]
        total = jnp.concatenate(tiles, axis=0)
        tall = total.reshape(height // 8, 8, cols)
        stage_ref[:, 0, k * 4 : (k + 1) * 4, :] = tall[:, :4]
        stage_ref[:, 1, k * 4 : (k + 1) * 4, :] = tall[:, 4:]
        straight = total.T
        for m in range(2):
            p = 2 * k + m
            wide = straight[m * half : (m + 1) * half].reshape(half // 8, 8, height)
            direct_ref[:, 0, p * 4 : (p + 1) * 4, :] = wide[:, :4]
            direct_ref[:, 1, p * 4 : (p + 1) * 4, :] = wide[:, 4:]
    mirror_ref[...] = stage_ref[...].astype(jnp.bfloat16)


def reduce_call(mask, pieces):
    sources, height, width = pieces.shape
    cols = 128
    vmem = pl.BlockSpec(memory_space=pltpu.VMEM)
    groups = width // cols
    return pl.pallas_call(
        reduce_kernel,
        in_specs=[pl.BlockSpec(memory_space=pltpu.SMEM), vmem],
        out_specs=[vmem, vmem],
        out_shape=[
            jax.ShapeDtypeStruct((cols // 16, 2, groups * 8, height), jnp.float32),
            jax.ShapeDtypeStruct((height // 8, 2, groups * 4, cols), jnp.bfloat16),
        ],
        scratch_shapes=[pltpu.VMEM((height // 8, 2, groups * 4, cols), jnp.float32)],
        compiler_params=params(),
    )(mask, pieces)


def align_kernel(direct_ref, out_ref, rows_ref):
    height, width = out_ref.shape
    sources, _, cols = direct_ref.shape
    blocks, pack = width // cols, cols // height
    own_rows = cols // (2 * sources)
    for g in range(sources // pack):
        turned = direct_ref[g * pack : (g + 1) * pack].reshape(cols, cols).T
        for m in range(pack):
            at = (g * pack + m) * own_rows
            tall = turned[:, m * height : (m + 1) * height].reshape(blocks, 2 * own_rows, height)
            rows_ref[:, 0, at : at + own_rows, :] = tall[:, :own_rows]
            rows_ref[:, 1, at : at + own_rows, :] = tall[:, own_rows:]
    for k in range(blocks):
        out_ref[:, k * cols : (k + 1) * cols] = rows_ref[k].reshape(cols, height).T


def align_call(direct):
    sources, height, cols = direct.shape
    width = sources * cols
    vmem = pl.BlockSpec(memory_space=pltpu.VMEM)
    return pl.pallas_call(
        align_kernel,
        in_specs=[vmem],
        out_specs=vmem,
        out_shape=jax.ShapeDtypeStruct((height, width), jnp.float32),
        scratch_shapes=[pltpu.VMEM((width // cols, 2, cols // 2, height), jnp.float32)],
        compiler_params=params(),
    )(direct)


def combine_kernel(partner_ref, direct_ref, mirror_ref, out_ref):
    pair_count, own_rows, width = out_ref.shape
    cols = mirror_ref.shape[2]
    blocks = width // cols
    mirror = mirror_ref[...].astype(jnp.float32).reshape(blocks, 2, mirror_ref.shape[1], cols)
    early, late = mirror[:, 0], mirror[:, 1]
    front = lax.broadcasted_iota(jnp.int32, early.shape, 2) < cols // 2
    plain = jnp.where(front, early, swing(late, 2))
    moved = jnp.where(front, swing(early, 2), late)
    for p in range(pair_count):
        mate = partner_ref[p]
        chosen = jnp.where(lax.rem(mate, 2) == 1, moved, plain)
        picked = chosen[:, :own_rows]
        for k in range(1, pair_count // 2):
            picked = jnp.where(mate // 2 == k, chosen[:, k * own_rows : (k + 1) * own_rows], picked)
        for k in range(blocks):
            span = slice(k * cols, (k + 1) * cols)
            out_ref[p, :, span] = direct_ref[p * own_rows : (p + 1) * own_rows, span] + picked[k]


def combine_call(partner, direct, mirror, pair_count):
    height, width = direct.shape
    vmem = pl.BlockSpec(memory_space=pltpu.VMEM)
    return pl.pallas_call(
        combine_kernel,
        in_specs=[pl.BlockSpec(memory_space=pltpu.SMEM), vmem, vmem],
        out_specs=vmem,
        out_shape=jax.ShapeDtypeStruct((pair_count, height // pair_count, width), jnp.float32),
        compiler_params=params(),
    )(partner, direct, mirror)


def turn(count, step):
    return [(i, (i + step) % count) for i in range(count)]


def on_device(amplitudes, factors, amp_mask, out_mask, partner):
    pair_count, amp_rows, amp_cols = amplitudes.shape
    batch_count, block_rows, full_width = factors.shape
    ring = 6
    first, second = prepare_call(amp_mask, amplitudes, factors, ring, 8)
    near = lax.all_to_all(second, "y", split_axis=0, concat_axis=0)
    units = lax.all_gather(gate_call(lax.all_gather(first, "zh", axis=0), near), "y", axis=0)

    back = lax.ppermute(near, "zh", turn(4, 1))
    ahead = lax.ppermute(near, "zh", turn(4, -1))
    left = lax.ppermute(back[:4], "zh", turn(4, 1))
    right = lax.ppermute(ahead[4:], "zh", turn(4, -1))

    early = early_call(factors, (near, back, ahead))
    late = late_call(factors, (left, right), early)
    flat = flat_call(factors, units)
    swapped = lax.ppermute(ladder_call(1, late, flat, units, jnp.bfloat16), "core", turn(2, 1))
    keep = ladder_call(0, late, flat, units, jnp.float32)
    partial = gather_call(keep, swapped, 8)
    pieces = lax.all_to_all(partial, ("zl", "x"), split_axis=0, concat_axis=0)
    direct, mirror = reduce_call(out_mask, pieces)
    mirror = lax.all_to_all(mirror.reshape(32, 16, 128), COL, split_axis=0, concat_axis=0)
    direct = lax.all_to_all(direct.reshape(16, 32, 128), ROW, split_axis=0, concat_axis=0)
    return combine_call(partner, align_call(direct), mirror, pair_count)


def solution(mesh):
    fine = Mesh(mesh.devices.reshape(2, 4, 2, 4, 8), ALL)
    return jax.shard_map(
        on_device,
        mesh=fine,
        in_specs=(P(None, COL, ROW), P(None, COL, None), P(), P(), P()),
        out_specs=P(None, COL + ROW, None),
        check_vma=False,
    )
```

```python
import functools

import jax
import jax.numpy as jnp
from jax import lax
from jax.experimental import pallas as pl
from jax.experimental.pallas import tpu as pltpu
from jax.sharding import Mesh, PartitionSpec as P

ROW = ("zl", "x", "core")
COL = ("zh", "y")
ALL = ROW + COL
MIB = 1024 * 1024


def params(mib=16):
    return pltpu.CompilerParams(vmem_limit_bytes=mib * MIB)


def place(names):
    at = lax.axis_index(names[0])
    for name in names[1:]:
        at = at * lax.axis_size(name) + lax.axis_index(name)
    return at


def prepare_kernel(mask_ref, amps_ref, factor_ref, first_ref, second_ref, masked_ref, slice_ref, order_ref, sems):
    batch_count, (copies, ring) = factor_ref.shape[0], second_ref.shape[:2]
    r = place(ROW)
    cols = amps_ref.shape[2]
    load = pltpu.make_async_copy(amps_ref, masked_ref, sems.at[0])
    load.start()
    block = factor_ref.at[:, :, pl.ds(pl.multiple_of(r * cols, cols), cols)]
    fetch = pltpu.make_async_copy(block, slice_ref, sems.at[1])
    fetch.start()
    weight = mask_ref[place(COL) // 2, r].astype(jnp.float32).astype(jnp.bfloat16)
    load.wait()
    masked_ref[...] = masked_ref[...] * weight
    stores = [pltpu.make_async_copy(masked_ref.at[ring:], first_ref.at[batch_count:], sems.at[2])]
    for k in range(copies):
        stores.append(pltpu.make_async_copy(masked_ref.at[:ring], second_ref.at[k], sems.at[4 + k]))
    for store in stores:
        store.start()
    fetch.wait()
    rows = slice_ref[...].astype(jnp.float32)
    half = rows.shape[1] // 2
    for k in range(half // 4):
        for core in range(2):
            at = core * half + k * 4
            order_ref[:, at : at + 4, :] = rows[:, (2 * k + core) * 4 : (2 * k + core + 1) * 4, :]
    slice_ref[...] = order_ref[...].astype(jnp.bfloat16)
    stores.append(pltpu.make_async_copy(slice_ref, first_ref.at[:batch_count], sems.at[3]))
    stores[-1].start()
    for store in stores:
        store.wait()


def prepare_call(mask, amplitudes, factors, ring, copies):
    pair_count, rows, cols = amplitudes.shape
    flat = factors.shape[0] + pair_count - ring
    hbm = pl.BlockSpec(memory_space=pltpu.HBM)
    return pl.pallas_call(
        prepare_kernel,
        in_specs=[pl.BlockSpec(memory_space=pltpu.SMEM), hbm, hbm],
        out_specs=[hbm, hbm],
        out_shape=[
            jax.ShapeDtypeStruct((flat, rows, cols), jnp.bfloat16),
            jax.ShapeDtypeStruct((copies, ring, rows, cols), jnp.bfloat16),
        ],
        scratch_shapes=[
            pltpu.VMEM(amplitudes.shape, jnp.bfloat16),
            pltpu.VMEM((factors.shape[0], rows, cols), jnp.bfloat16),
            pltpu.VMEM((factors.shape[0], rows, cols), jnp.float32),
            pltpu.SemaphoreType.DMA((4 + copies,)),
        ],
        compiler_params=params(60),
    )(mask, amplitudes, factors)


def gate_kernel(held_ref, other_ref, out_ref):
    pass


def gate_call(held, other):
    anywhere = pl.BlockSpec(memory_space=pl.ANY)
    return pl.pallas_call(
        gate_kernel,
        in_specs=[anywhere, anywhere],
        out_specs=anywhere,
        out_shape=jax.ShapeDtypeStruct(held.shape, held.dtype),
        input_output_aliases={0: 0},
        compiler_params=params(),
    )(held, other)


def spread_product(product, out_ref, first, batch_count, block_rows):
    cols = out_ref.shape[0] // batch_count
    for pair in range(product.shape[1] // cols // 2):
        for q in range(batch_count):
            rows = product[q * block_rows : (q + 1) * block_rows, 2 * pair * cols : 2 * (pair + 1) * cols]
            block = jnp.concatenate([rows[:, :cols], rows[:, cols:]], axis=0)
            at = first + 2 * pair * block_rows
            out_ref[q * cols : (q + 1) * cols, at : at + 2 * block_rows] = block.T.astype(jnp.bfloat16)


def ring_term(own_ref, blocks, move):
    batch_count, block_rows, width = own_ref.shape
    group = width // 4
    at = pl.multiple_of(lax.rem(lax.axis_index("zh") + move, 4) * group, group)
    own = own_ref[:, :, pl.ds(at, group)].reshape(batch_count * block_rows, group)
    lanes = [
        jnp.concatenate([ref[k, p] for ref in blocks for k in range(ref.shape[0])], axis=0)
        for p in range(blocks[0].shape[1])
    ]
    return jnp.dot(own, jnp.concatenate(lanes, axis=1), preferred_element_type=jnp.float32)


def early_kernel(own_ref, near_ref, back_ref, ahead_ref, out_ref):
    step = 1 + 2 * lax.axis_index("zl")
    product = ring_term(own_ref, [near_ref], 0)
    product = product + ring_term(own_ref, [back_ref], 4 - step)
    out_ref[...] = product + ring_term(own_ref, [ahead_ref], step)


def early_call(own, parts):
    batch_count, block_rows, width = own.shape
    pair_count, rows, cols = parts[0].shape[1:]
    return pl.pallas_call(
        early_kernel,
        grid=(pair_count // 2,),
        in_specs=[pl.BlockSpec(memory_space=pltpu.VMEM)]
        + [pl.BlockSpec((part.shape[0], 2, rows, cols), lambda i: (0, i, 0, 0)) for part in parts],
        out_specs=pl.BlockSpec((batch_count * block_rows, 2 * cols), lambda i: (0, i)),
        out_shape=jax.ShapeDtypeStruct((batch_count * block_rows, pair_count * cols), jnp.float32),
        compiler_params=params(),
    )(own, *parts)


def late_kernel(own_ref, left_ref, right_ref, early_ref, out_ref):
    batch_count, block_rows, width = own_ref.shape
    product = early_ref[...] + ring_term(own_ref, [left_ref, right_ref], 2)
    spread_product(product, out_ref, 0, batch_count, block_rows)


def late_call(own, parts, early):
    batch_count, block_rows, width = own.shape
    pair_count, rows, cols = parts[0].shape[1:]
    vmem = pl.BlockSpec(memory_space=pltpu.VMEM)
    return pl.pallas_call(
        late_kernel,
        in_specs=[vmem] * 4,
        out_specs=vmem,
        out_shape=jax.ShapeDtypeStruct((batch_count * cols, pair_count * block_rows), jnp.bfloat16),
        compiler_params=params(),
    )(own, *parts, early)


def flat_kernel(own_ref, units_ref, out_ref, amps_ref, sems):
    batch_count, block_rows, width = own_ref.shape
    y_count, z_count, pairs, rows, cols = amps_ref.shape
    loads = []
    for p in range(pairs):
        block = units_ref.at[:, :, batch_count + p]
        loads.append(pltpu.make_async_copy(block, amps_ref.at[:, :, p], sems.at[p]))
        loads[p].start()
    lanes = []
    for p in range(pairs):
        loads[p].wait()
        lanes.append(jnp.concatenate([amps_ref[y, z, p] for z in range(z_count) for y in range(y_count)], axis=0))
    own = own_ref[...].reshape(batch_count * block_rows, width)
    product = jnp.dot(own, jnp.concatenate(lanes, axis=1), preferred_element_type=jnp.float32)
    spread_product(product, out_ref, 0, batch_count, block_rows)


def flat_call(own, units):
    batch_count, block_rows, width = own.shape
    y_count, z_count, unit_count, rows, cols = units.shape
    pairs = unit_count - batch_count
    vmem = pl.BlockSpec(memory_space=pltpu.VMEM)
    return pl.pallas_call(
        flat_kernel,
        in_specs=[vmem, pl.BlockSpec(memory_space=pltpu.HBM)],
        out_specs=vmem,
        out_shape=jax.ShapeDtypeStruct((batch_count * cols, pairs * block_rows), jnp.bfloat16),
        scratch_shapes=[
            pltpu.VMEM((y_count, z_count, pairs, rows, cols), jnp.bfloat16),
            pltpu.SemaphoreType.DMA((pairs,)),
        ],
        compiler_params=params(48),
    )(own, units)


def ladder_kernel(flip, ring_ref, flat_ref, units_ref, out_ref, block_ref, sems):
    y_count, z_count, batch_count, rows, cols = block_ref.shape
    side = lax.rem(lax.axis_index("core") + flip, 2)
    step = z_count // 2
    here = pl.ds(pl.multiple_of(side * rows, rows), rows)
    loads = []
    for k in range(2):
        span = pl.ds(k * step, step)
        source = units_ref.at[:, span, pl.ds(0, batch_count), here]
        loads.append(pltpu.make_async_copy(source, block_ref.at[:, span], sems.at[k]))
        loads[-1].start()
    inner = jnp.concatenate([ring_ref[...], flat_ref[...]], axis=1)
    height = step * y_count * rows
    for k in range(2):
        loads[k].wait()
        places = [(z, y) for z in range(k * step, (k + 1) * step) for y in range(y_count)]
        lanes = [jnp.concatenate([block_ref[y, z, q] for z, y in places], axis=0) for q in range(batch_count)]
        factor = jnp.concatenate(lanes, axis=1)
        product = jnp.dot(factor, inner, preferred_element_type=jnp.float32)
        out_ref[k * height : (k + 1) * height] = product.astype(out_ref.dtype)


def ladder_call(flip, ring, flat, units, kind):
    depth, width = ring.shape[0], ring.shape[1] + flat.shape[1]
    y_count, z_count, unit_count, rows, cols = units.shape
    vmem = pl.BlockSpec(memory_space=pltpu.VMEM)
    return pl.pallas_call(
        functools.partial(ladder_kernel, flip),
        in_specs=[vmem, vmem, pl.BlockSpec(memory_space=pltpu.HBM)],
        out_specs=vmem,
        out_shape=jax.ShapeDtypeStruct((y_count * z_count * rows // 2, width), kind),
        scratch_shapes=[
            pltpu.VMEM((y_count, z_count, depth // cols, rows // 2, cols), jnp.bfloat16),
            pltpu.SemaphoreType.DMA((2,)),
        ],
        compiler_params=params(48),
    )(ring, flat, units)


def swing(block, axis):
    half = block.shape[axis] // 2
    first = lax.slice_in_dim(block, 0, half, axis=axis)
    return jnp.concatenate([lax.slice_in_dim(block, half, 2 * half, axis=axis), first], axis=axis)


def gather_kernel(keep_ref, other_ref, out_ref):
    groups, height, cols = out_ref.shape
    total = keep_ref[...] + other_ref[...].astype(jnp.float32)
    tiles = total.reshape(height // 8, 2, groups // 2, 8, cols)
    top = lax.broadcasted_iota(jnp.int32, (height // 8, 8, cols), 1) < 4
    for k in range(groups // 2):
        first, second = tiles[:, 0, k], tiles[:, 1, k]
        even = jnp.where(top, first, swing(second, 1))
        odd = jnp.where(top, swing(first, 1), second)
        out_ref[2 * k] = even.reshape(height, cols).astype(jnp.bfloat16)
        out_ref[2 * k + 1] = odd.reshape(height, cols).astype(jnp.bfloat16)


def gather_call(keep, other, groups):
    height, width = keep.shape
    cols = 128
    return pl.pallas_call(
        gather_kernel,
        grid=(width // cols,),
        in_specs=[pl.BlockSpec((height, cols), lambda i: (0, i))] * 2,
        out_specs=pl.BlockSpec((groups, height // groups, cols), lambda i: (0, 0, i)),
        out_shape=jax.ShapeDtypeStruct((groups, height // groups, width), jnp.bfloat16),
        compiler_params=params(),
    )(keep, other)


def reduce_kernel(mask_ref, part_ref, direct_ref, mirror_ref, stage_ref):
    sources, height, width = part_ref.shape
    cols = direct_ref.shape[3]
    half = cols // 2
    row = place(COL) // 2
    for k in range(width // cols):
        span = slice(k * cols, (k + 1) * cols)
        total = part_ref[0, :, span].astype(jnp.float32)
        for m in range(1, sources):
            total = total + part_ref[m, :, span].astype(jnp.float32)
        tiles = [total[t * 8 : (t + 1) * 8] * mask_ref[row, t].astype(jnp.float32) for t in range(height // 8)]
        total = jnp.concatenate(tiles, axis=0)
        tall = total.reshape(height // 8, 8, cols)
        stage_ref[:, 0, k * 4 : (k + 1) * 4, :] = tall[:, :4]
        stage_ref[:, 1, k * 4 : (k + 1) * 4, :] = tall[:, 4:]
        straight = total.T
        for m in range(2):
            p = 2 * k + m
            wide = straight[m * half : (m + 1) * half].reshape(half // 8, 8, height)
            direct_ref[:, 0, p * 4 : (p + 1) * 4, :] = wide[:, :4]
            direct_ref[:, 1, p * 4 : (p + 1) * 4, :] = wide[:, 4:]
    mirror_ref[...] = stage_ref[...].astype(jnp.bfloat16)


def reduce_call(mask, pieces):
    sources, height, width = pieces.shape
    cols = 128
    vmem = pl.BlockSpec(memory_space=pltpu.VMEM)
    groups = width // cols
    return pl.pallas_call(
        reduce_kernel,
        in_specs=[pl.BlockSpec(memory_space=pltpu.SMEM), vmem],
        out_specs=[vmem, vmem],
        out_shape=[
            jax.ShapeDtypeStruct((cols // 16, 2, groups * 8, height), jnp.float32),
            jax.ShapeDtypeStruct((height // 8, 2, groups * 4, cols), jnp.bfloat16),
        ],
        scratch_shapes=[pltpu.VMEM((height // 8, 2, groups * 4, cols), jnp.float32)],
        compiler_params=params(),
    )(mask, pieces)


def align_kernel(direct_ref, out_ref, rows_ref):
    height, width = out_ref.shape
    sources, _, cols = direct_ref.shape
    blocks, pack = width // cols, cols // height
    own_rows = cols // (2 * sources)
    for g in range(sources // pack):
        turned = direct_ref[g * pack : (g + 1) * pack].reshape(cols, cols).T
        for m in range(pack):
            at = (g * pack + m) * own_rows
            tall = turned[:, m * height : (m + 1) * height].reshape(blocks, 2 * own_rows, height)
            rows_ref[:, 0, at : at + own_rows, :] = tall[:, :own_rows]
            rows_ref[:, 1, at : at + own_rows, :] = tall[:, own_rows:]
    for k in range(blocks):
        out_ref[:, k * cols : (k + 1) * cols] = rows_ref[k].reshape(cols, height).T


def align_call(direct):
    sources, height, cols = direct.shape
    width = sources * cols
    vmem = pl.BlockSpec(memory_space=pltpu.VMEM)
    return pl.pallas_call(
        align_kernel,
        in_specs=[vmem],
        out_specs=vmem,
        out_shape=jax.ShapeDtypeStruct((height, width), jnp.float32),
        scratch_shapes=[pltpu.VMEM((width // cols, 2, cols // 2, height), jnp.float32)],
        compiler_params=params(),
    )(direct)


def combine_kernel(partner_ref, direct_ref, mirror_ref, out_ref):
    pair_count, own_rows, width = out_ref.shape
    cols = mirror_ref.shape[2]
    blocks = width // cols
    mirror = mirror_ref[...].astype(jnp.float32).reshape(blocks, 2, mirror_ref.shape[1], cols)
    early, late = mirror[:, 0], mirror[:, 1]
    front = lax.broadcasted_iota(jnp.int32, early.shape, 2) < cols // 2
    plain = jnp.where(front, early, swing(late, 2))
    moved = jnp.where(front, swing(early, 2), late)
    for p in range(pair_count):
        mate = partner_ref[p]
        chosen = jnp.where(lax.rem(mate, 2) == 1, moved, plain)
        picked = chosen[:, :own_rows]
        for k in range(1, pair_count // 2):
            picked = jnp.where(mate // 2 == k, chosen[:, k * own_rows : (k + 1) * own_rows], picked)
        for k in range(blocks):
            span = slice(k * cols, (k + 1) * cols)
            out_ref[p, :, span] = direct_ref[p * own_rows : (p + 1) * own_rows, span] + picked[k]


def combine_call(partner, direct, mirror, pair_count):
    height, width = direct.shape
    vmem = pl.BlockSpec(memory_space=pltpu.VMEM)
    return pl.pallas_call(
        combine_kernel,
        in_specs=[pl.BlockSpec(memory_space=pltpu.SMEM), vmem, vmem],
        out_specs=vmem,
        out_shape=jax.ShapeDtypeStruct((pair_count, height // pair_count, width), jnp.float32),
        compiler_params=params(),
    )(partner, direct, mirror)


def turn(count, step):
    return [(i, (i + step) % count) for i in range(count)]


def cross(step):
    return [(k, k // 4 * 4 + (k % 4 + (1 - k // 4 * 2) * step) % 4) for k in range(8)]


def on_device(amplitudes, factors, amp_mask, out_mask, partner):
    pair_count, amp_rows, amp_cols = amplitudes.shape
    batch_count, block_rows, full_width = factors.shape
    ring = 6
    first, second = prepare_call(amp_mask, amplitudes, factors, ring, 8)
    near = lax.all_to_all(second, "y", split_axis=0, concat_axis=0)
    units = lax.all_gather(gate_call(lax.all_gather(first, "zh", axis=0), near), "y", axis=0)

    back = lax.ppermute(near, ("zl", "zh"), cross(1))
    ahead = lax.ppermute(near, ("zl", "zh"), cross(-1))
    left = lax.ppermute(back[:4], ("zl", "zh"), cross(1))
    right = lax.ppermute(ahead[4:], ("zl", "zh"), cross(-1))

    early = early_call(factors, (near, back, ahead))
    late = late_call(factors, (left, right), early)
    flat = flat_call(factors, units)
    swapped = lax.ppermute(ladder_call(1, late, flat, units, jnp.bfloat16), "core", turn(2, 1))
    keep = ladder_call(0, late, flat, units, jnp.float32)
    partial = gather_call(keep, swapped, 8)
    pieces = lax.all_to_all(partial, ("zl", "x"), split_axis=0, concat_axis=0)
    direct, mirror = reduce_call(out_mask, pieces)
    mirror = lax.all_to_all(mirror.reshape(32, 16, 128), COL, split_axis=0, concat_axis=0)
    direct = lax.all_to_all(direct.reshape(16, 32, 128), ROW, split_axis=0, concat_axis=0)
    return combine_call(partner, align_call(direct), mirror, pair_count)


def solution(mesh):
    fine = Mesh(mesh.devices.reshape(2, 4, 2, 4, 8), ALL)
    return jax.shard_map(
        on_device,
        mesh=fine,
        in_specs=(P(None, COL, ROW), P(None, COL, None), P(), P(), P()),
        out_specs=P(None, COL + ROW, None),
        check_vma=False,
    )
```

```python
import functools

import jax
import jax.numpy as jnp
from jax import lax
from jax.experimental import pallas as pl
from jax.experimental.pallas import tpu as pltpu
from jax.sharding import Mesh, PartitionSpec as P

ROW = ("zl", "x", "core")
COL = ("zh", "y")
ALL = ROW + COL
MIB = 1024 * 1024


def params(mib=16):
    return pltpu.CompilerParams(vmem_limit_bytes=mib * MIB)


def place(names):
    at = lax.axis_index(names[0])
    for name in names[1:]:
        at = at * lax.axis_size(name) + lax.axis_index(name)
    return at


def prepare_kernel(mask_ref, amps_ref, factor_ref, first_ref, second_ref, masked_ref, slice_ref, order_ref, sems):
    batch_count, (copies, ring) = factor_ref.shape[0], second_ref.shape[:2]
    r = place(ROW)
    cols = amps_ref.shape[2]
    load = pltpu.make_async_copy(amps_ref, masked_ref, sems.at[0])
    load.start()
    block = factor_ref.at[:, :, pl.ds(pl.multiple_of(r * cols, cols), cols)]
    fetch = pltpu.make_async_copy(block, slice_ref, sems.at[1])
    fetch.start()
    weight = mask_ref[place(COL) // 2, r].astype(jnp.float32).astype(jnp.bfloat16)
    load.wait()
    masked_ref[...] = masked_ref[...] * weight
    stores = [pltpu.make_async_copy(masked_ref.at[ring:], first_ref.at[batch_count:], sems.at[2])]
    for k in range(copies):
        stores.append(pltpu.make_async_copy(masked_ref.at[:ring], second_ref.at[k], sems.at[4 + k]))
    for store in stores:
        store.start()
    fetch.wait()
    rows = slice_ref[...].astype(jnp.float32)
    half = rows.shape[1] // 2
    for k in range(half // 4):
        for core in range(2):
            at = core * half + k * 4
            order_ref[:, at : at + 4, :] = rows[:, (2 * k + core) * 4 : (2 * k + core + 1) * 4, :]
    slice_ref[...] = order_ref[...].astype(jnp.bfloat16)
    stores.append(pltpu.make_async_copy(slice_ref, first_ref.at[:batch_count], sems.at[3]))
    stores[-1].start()
    for store in stores:
        store.wait()


def prepare_call(mask, amplitudes, factors, ring, copies):
    pair_count, rows, cols = amplitudes.shape
    flat = factors.shape[0] + pair_count - ring
    hbm = pl.BlockSpec(memory_space=pltpu.HBM)
    return pl.pallas_call(
        prepare_kernel,
        in_specs=[pl.BlockSpec(memory_space=pltpu.SMEM), hbm, hbm],
        out_specs=[hbm, hbm],
        out_shape=[
            jax.ShapeDtypeStruct((flat, rows, cols), jnp.bfloat16),
            jax.ShapeDtypeStruct((copies, ring, rows, cols), jnp.bfloat16),
        ],
        scratch_shapes=[
            pltpu.VMEM(amplitudes.shape, jnp.bfloat16),
            pltpu.VMEM((factors.shape[0], rows, cols), jnp.bfloat16),
            pltpu.VMEM((factors.shape[0], rows, cols), jnp.float32),
            pltpu.SemaphoreType.DMA((4 + copies,)),
        ],
        compiler_params=params(60),
    )(mask, amplitudes, factors)


def gate_kernel(held_ref, other_ref, out_ref):
    pass


def gate_call(held, other):
    anywhere = pl.BlockSpec(memory_space=pl.ANY)
    return pl.pallas_call(
        gate_kernel,
        in_specs=[anywhere, anywhere],
        out_specs=anywhere,
        out_shape=jax.ShapeDtypeStruct(held.shape, held.dtype),
        input_output_aliases={0: 0},
        compiler_params=params(),
    )(held, other)


def spread_product(product, out_ref, first, batch_count, block_rows):
    cols = out_ref.shape[0] // batch_count
    for pair in range(product.shape[1] // cols // 2):
        for q in range(batch_count):
            rows = product[q * block_rows : (q + 1) * block_rows, 2 * pair * cols : 2 * (pair + 1) * cols]
            block = jnp.concatenate([rows[:, :cols], rows[:, cols:]], axis=0)
            at = first + 2 * pair * block_rows
            out_ref[q * cols : (q + 1) * cols, at : at + 2 * block_rows] = block.T.astype(jnp.bfloat16)


def ring_term(own_ref, blocks, move):
    batch_count, block_rows, width = own_ref.shape
    group = width // 4
    at = pl.multiple_of(lax.rem(lax.axis_index("zh") + move, 4) * group, group)
    own = own_ref[:, :, pl.ds(at, group)].reshape(batch_count * block_rows, group)
    lanes = [
        jnp.concatenate([ref[k, p] for ref in blocks for k in range(ref.shape[0])], axis=0)
        for p in range(blocks[0].shape[1])
    ]
    return jnp.dot(own, jnp.concatenate(lanes, axis=1), preferred_element_type=jnp.float32)


def early_kernel(own_ref, near_ref, back_ref, ahead_ref, out_ref):
    step = 1 + 2 * lax.axis_index("zl")
    product = ring_term(own_ref, [near_ref], 0)
    product = product + ring_term(own_ref, [back_ref], 4 - step)
    out_ref[...] = product + ring_term(own_ref, [ahead_ref], step)


def early_call(own, parts):
    batch_count, block_rows, width = own.shape
    pair_count, rows, cols = parts[0].shape[1:]
    return pl.pallas_call(
        early_kernel,
        grid=(pair_count // 2,),
        in_specs=[pl.BlockSpec(memory_space=pltpu.VMEM)]
        + [pl.BlockSpec((part.shape[0], 2, rows, cols), lambda i: (0, i, 0, 0)) for part in parts],
        out_specs=pl.BlockSpec((batch_count * block_rows, 2 * cols), lambda i: (0, i)),
        out_shape=jax.ShapeDtypeStruct((batch_count * block_rows, pair_count * cols), jnp.float32),
        compiler_params=params(),
    )(own, *parts)


def late_kernel(own_ref, left_ref, right_ref, early_ref, out_ref):
    batch_count, block_rows, width = own_ref.shape
    product = early_ref[...] + ring_term(own_ref, [left_ref, right_ref], 2)
    spread_product(product, out_ref, 0, batch_count, block_rows)


def late_call(own, parts, early, total):
    batch_count, block_rows, width = own.shape
    pair_count, rows, cols = parts[0].shape[1:]
    vmem = pl.BlockSpec(memory_space=pltpu.VMEM)
    return pl.pallas_call(
        late_kernel,
        in_specs=[vmem] * 4,
        out_specs=vmem,
        out_shape=jax.ShapeDtypeStruct((batch_count * cols, total * block_rows), jnp.bfloat16),
        compiler_params=params(),
    )(own, *parts, early)


GATED = 1
RING = ((0, 0, 4), (-1, 0, 4), (1, 0, 4), (-2, 0, 4), (2, 0, 4), (-3, 0, 4), (3, 0, 4), (4, 0, 2), (4, 2, 4))


def ring_place(move):
    return lax.rem(lax.axis_index("y") + 8 + move, 8)


def flat_kernel(own_ref, held_ref, *refs):
    pieces, (out_ref, amps_ref, sems) = refs[: len(RING)], refs[len(RING) :]
    batch_count, block_rows, width = own_ref.shape
    y_count, z_count, pairs, rows, cols = amps_ref.shape
    loads = []
    for k, (move, first, last) in enumerate(RING):
        target = amps_ref.at[ring_place(move), pl.ds(first, last - first)]
        loads.append(pltpu.make_async_copy(pieces[k].at[:, pl.ds(batch_count, pairs)], target, sems.at[k]))
        loads[k].start()
    for load in loads:
        load.wait()
    lanes = [
        jnp.concatenate([amps_ref[y, z, p] for z in range(z_count) for y in range(y_count)], axis=0)
        for p in range(pairs)
    ]
    own = own_ref[...].reshape(batch_count * block_rows, width)
    product = jnp.dot(own, jnp.concatenate(lanes, axis=1), preferred_element_type=jnp.float32)
    spread_product(product, out_ref, out_ref.shape[1] - pairs * block_rows, batch_count, block_rows)


def flat_call(own, pieces, inner):
    batch_count, block_rows, width = own.shape
    z_count, unit_count, rows, cols = pieces[0].shape
    pairs = unit_count - batch_count
    vmem = pl.BlockSpec(memory_space=pltpu.VMEM)
    return pl.pallas_call(
        flat_kernel,
        in_specs=[vmem, vmem] + [pl.BlockSpec(memory_space=pl.ANY)] * len(pieces),
        out_specs=vmem,
        out_shape=jax.ShapeDtypeStruct(inner.shape, jnp.bfloat16),
        input_output_aliases={1: 0},
        scratch_shapes=[
            pltpu.VMEM((8, z_count, pairs, rows, cols), jnp.bfloat16),
            pltpu.SemaphoreType.DMA((len(pieces),)),
        ],
        compiler_params=params(),
    )(own, inner, *pieces)


def ladder_kernel(flip, inner_ref, *refs):
    pieces, (out_ref, block_ref, sems) = refs[: len(RING)], refs[len(RING) :]
    y_count, z_count, batch_count, rows, cols = block_ref.shape
    side = lax.rem(lax.axis_index("core") + flip, 2)
    step = z_count // 2
    here = pl.ds(pl.multiple_of(side * rows, rows), rows)
    loads = ([], [])
    for k in range(2):
        for m, (move, first, last) in enumerate(RING):
            if first <= k * step < last:
                source = pieces[m].at[pl.ds(k * step - first, step), pl.ds(0, batch_count), here]
                target = block_ref.at[ring_place(move), pl.ds(k * step, step)]
                loads[k].append(pltpu.make_async_copy(source, target, sems.at[k, m]))
                loads[k][-1].start()
    height = step * y_count * rows
    for k in range(2):
        for load in loads[k]:
            load.wait()
        places = [(z, y) for z in range(k * step, (k + 1) * step) for y in range(y_count)]
        lanes = [jnp.concatenate([block_ref[y, z, q] for z, y in places], axis=0) for q in range(batch_count)]
        factor = jnp.concatenate(lanes, axis=1)
        product = jnp.dot(factor, inner_ref[...], preferred_element_type=jnp.float32)
        out_ref[k * height : (k + 1) * height] = product.astype(out_ref.dtype)


def ladder_call(flip, inner, pieces, kind):
    depth, width = inner.shape
    z_count, unit_count, rows, cols = pieces[0].shape
    vmem = pl.BlockSpec(memory_space=pltpu.VMEM)
    return pl.pallas_call(
        functools.partial(ladder_kernel, flip),
        in_specs=[vmem] + [pl.BlockSpec(memory_space=pl.ANY)] * len(pieces),
        out_specs=vmem,
        out_shape=jax.ShapeDtypeStruct((8 * z_count * rows // 2, width), kind),
        scratch_shapes=[
            pltpu.VMEM((8, z_count, depth // cols, rows // 2, cols), jnp.bfloat16),
            pltpu.SemaphoreType.DMA((2, len(pieces))),
        ],
        compiler_params=params(),
    )(inner, *pieces)


def swing(block, axis):
    half = block.shape[axis] // 2
    first = lax.slice_in_dim(block, 0, half, axis=axis)
    return jnp.concatenate([lax.slice_in_dim(block, half, 2 * half, axis=axis), first], axis=axis)


def gather_kernel(keep_ref, other_ref, out_ref):
    groups, height, cols = out_ref.shape
    total = keep_ref[...] + other_ref[...].astype(jnp.float32)
    tiles = total.reshape(height // 8, 2, groups // 2, 8, cols)
    top = lax.broadcasted_iota(jnp.int32, (height // 8, 8, cols), 1) < 4
    for k in range(groups // 2):
        first, second = tiles[:, 0, k], tiles[:, 1, k]
        even = jnp.where(top, first, swing(second, 1))
        odd = jnp.where(top, swing(first, 1), second)
        out_ref[2 * k] = even.reshape(height, cols).astype(jnp.bfloat16)
        out_ref[2 * k + 1] = odd.reshape(height, cols).astype(jnp.bfloat16)


def gather_call(keep, other, groups):
    height, width = keep.shape
    cols = 128
    return pl.pallas_call(
        gather_kernel,
        grid=(width // cols,),
        in_specs=[pl.BlockSpec((height, cols), lambda i: (0, i))] * 2,
        out_specs=pl.BlockSpec((groups, height // groups, cols), lambda i: (0, 0, i)),
        out_shape=jax.ShapeDtypeStruct((groups, height // groups, width), jnp.bfloat16),
        compiler_params=params(),
    )(keep, other)


def reduce_kernel(mask_ref, part_ref, direct_ref, mirror_ref, stage_ref):
    sources, height, width = part_ref.shape
    cols = direct_ref.shape[3]
    half = cols // 2
    row = place(COL) // 2
    for k in range(width // cols):
        span = slice(k * cols, (k + 1) * cols)
        total = part_ref[0, :, span].astype(jnp.float32)
        for m in range(1, sources):
            total = total + part_ref[m, :, span].astype(jnp.float32)
        tiles = [total[t * 8 : (t + 1) * 8] * mask_ref[row, t].astype(jnp.float32) for t in range(height // 8)]
        total = jnp.concatenate(tiles, axis=0)
        tall = total.reshape(height // 8, 8, cols)
        stage_ref[:, 0, k * 4 : (k + 1) * 4, :] = tall[:, :4]
        stage_ref[:, 1, k * 4 : (k + 1) * 4, :] = tall[:, 4:]
        straight = total.T
        for m in range(2):
            p = 2 * k + m
            wide = straight[m * half : (m + 1) * half].reshape(half // 8, 8, height)
            direct_ref[:, 0, p * 4 : (p + 1) * 4, :] = wide[:, :4]
            direct_ref[:, 1, p * 4 : (p + 1) * 4, :] = wide[:, 4:]
    mirror_ref[...] = stage_ref[...].astype(jnp.bfloat16)


def reduce_call(mask, pieces):
    sources, height, width = pieces.shape
    cols = 128
    vmem = pl.BlockSpec(memory_space=pltpu.VMEM)
    groups = width // cols
    return pl.pallas_call(
        reduce_kernel,
        in_specs=[pl.BlockSpec(memory_space=pltpu.SMEM), vmem],
        out_specs=[vmem, vmem],
        out_shape=[
            jax.ShapeDtypeStruct((cols // 16, 2, groups * 8, height), jnp.float32),
            jax.ShapeDtypeStruct((height // 8, 2, groups * 4, cols), jnp.bfloat16),
        ],
        scratch_shapes=[pltpu.VMEM((height // 8, 2, groups * 4, cols), jnp.float32)],
        compiler_params=params(),
    )(mask, pieces)


def align_kernel(direct_ref, out_ref, rows_ref):
    height, width = out_ref.shape
    sources, _, cols = direct_ref.shape
    blocks, pack = width // cols, cols // height
    own_rows = cols // (2 * sources)
    for g in range(sources // pack):
        turned = direct_ref[g * pack : (g + 1) * pack].reshape(cols, cols).T
        for m in range(pack):
            at = (g * pack + m) * own_rows
            tall = turned[:, m * height : (m + 1) * height].reshape(blocks, 2 * own_rows, height)
            rows_ref[:, 0, at : at + own_rows, :] = tall[:, :own_rows]
            rows_ref[:, 1, at : at + own_rows, :] = tall[:, own_rows:]
    for k in range(blocks):
        out_ref[:, k * cols : (k + 1) * cols] = rows_ref[k].reshape(cols, height).T


def align_call(direct):
    sources, height, cols = direct.shape
    width = sources * cols
    vmem = pl.BlockSpec(memory_space=pltpu.VMEM)
    return pl.pallas_call(
        align_kernel,
        in_specs=[vmem],
        out_specs=vmem,
        out_shape=jax.ShapeDtypeStruct((height, width), jnp.float32),
        scratch_shapes=[pltpu.VMEM((width // cols, 2, cols // 2, height), jnp.float32)],
        compiler_params=params(),
    )(direct)


def combine_kernel(partner_ref, direct_ref, mirror_ref, out_ref):
    pair_count, own_rows, width = out_ref.shape
    cols = mirror_ref.shape[2]
    blocks = width // cols
    mirror = mirror_ref[...].astype(jnp.float32).reshape(blocks, 2, mirror_ref.shape[1], cols)
    early, late = mirror[:, 0], mirror[:, 1]
    front = lax.broadcasted_iota(jnp.int32, early.shape, 2) < cols // 2
    plain = jnp.where(front, early, swing(late, 2))
    moved = jnp.where(front, swing(early, 2), late)
    for p in range(pair_count):
        mate = partner_ref[p]
        chosen = jnp.where(lax.rem(mate, 2) == 1, moved, plain)
        picked = chosen[:, :own_rows]
        for k in range(1, pair_count // 2):
            picked = jnp.where(mate // 2 == k, chosen[:, k * own_rows : (k + 1) * own_rows], picked)
        for k in range(blocks):
            span = slice(k * cols, (k + 1) * cols)
            out_ref[p, :, span] = direct_ref[p * own_rows : (p + 1) * own_rows, span] + picked[k]


def combine_call(partner, direct, mirror, pair_count):
    height, width = direct.shape
    vmem = pl.BlockSpec(memory_space=pltpu.VMEM)
    return pl.pallas_call(
        combine_kernel,
        in_specs=[pl.BlockSpec(memory_space=pltpu.SMEM), vmem, vmem],
        out_specs=vmem,
        out_shape=jax.ShapeDtypeStruct((pair_count, height // pair_count, width), jnp.float32),
        compiler_params=params(),
    )(partner, direct, mirror)


def turn(count, step):
    return [(i, (i + step) % count) for i in range(count)]


def cross(step):
    return [(k, k // 4 * 4 + (k % 4 + (1 - k // 4 * 2) * step) % 4) for k in range(8)]


def on_device(amplitudes, factors, amp_mask, out_mask, partner):
    pair_count, amp_rows, amp_cols = amplitudes.shape
    batch_count, block_rows, full_width = factors.shape
    ring = 6
    first, second = prepare_call(amp_mask, amplitudes, factors, ring, 8)
    near = lax.all_to_all(second, "y", split_axis=0, concat_axis=0)
    held = gate_call(lax.all_gather(first, "zh", axis=0), near)

    back = lax.ppermute(near, ("zl", "zh"), cross(1))
    ahead = lax.ppermute(near, ("zl", "zh"), cross(-1))
    left = lax.ppermute(back[:4], ("zl", "zh"), cross(1))
    right = lax.ppermute(ahead[4:], ("zl", "zh"), cross(-1))

    up, down = held, held
    units = [held]
    for k in range(3):
        up = lax.ppermute(up, "y", turn(8, 1))
        down = lax.ppermute(down, "y", turn(8, -1))
        if k == GATED:
            up, down = gate_call(up, back), gate_call(down, ahead)
        units += [up, down]
    units.append(lax.ppermute(up[:2], "y", turn(8, 1)))
    units.append(lax.ppermute(down[2:], "y", turn(8, -1)))

    early = early_call(factors, (near, back, ahead))
    late = late_call(factors, (left, right), early, pair_count)
    inner = flat_call(factors, units, late)
    swapped = lax.ppermute(ladder_call(1, inner, units, jnp.bfloat16), "core", turn(2, 1))
    keep = ladder_call(0, inner, units, jnp.float32)
    partial = gather_call(keep, swapped, 8)
    pieces = lax.all_to_all(partial, ("zl", "x"), split_axis=0, concat_axis=0)
    direct, mirror = reduce_call(out_mask, pieces)
    mirror = lax.all_to_all(mirror.reshape(32, 16, 128), COL, split_axis=0, concat_axis=0)
    direct = lax.all_to_all(direct.reshape(16, 32, 128), ROW, split_axis=0, concat_axis=0)
    return combine_call(partner, align_call(direct), mirror, pair_count)


def solution(mesh):
    fine = Mesh(mesh.devices.reshape(2, 4, 2, 4, 8), ALL)
    return jax.shard_map(
        on_device,
        mesh=fine,
        in_specs=(P(None, COL, ROW), P(None, COL, None), P(), P(), P()),
        out_specs=P(None, COL + ROW, None),
        check_vma=False,
    )
```

```python
import functools

import jax
import jax.numpy as jnp
from jax import lax
from jax.experimental import pallas as pl
from jax.experimental.pallas import tpu as pltpu
from jax.sharding import Mesh, PartitionSpec as P

ROW = ("zl", "x", "core")
COL = ("zh", "y")
ALL = ROW + COL
MIB = 1024 * 1024


def params(mib=16):
    return pltpu.CompilerParams(vmem_limit_bytes=mib * MIB)


def place(names):
    at = lax.axis_index(names[0])
    for name in names[1:]:
        at = at * lax.axis_size(name) + lax.axis_index(name)
    return at


def prepare_kernel(mask_ref, amps_ref, factor_ref, first_ref, second_ref, masked_ref, slice_ref, order_ref, sems):
    batch_count, (copies, ring) = factor_ref.shape[0], second_ref.shape[:2]
    r = place(ROW)
    cols = amps_ref.shape[2]
    load = pltpu.make_async_copy(amps_ref, masked_ref, sems.at[0])
    load.start()
    block = factor_ref.at[:, :, pl.ds(pl.multiple_of(r * cols, cols), cols)]
    fetch = pltpu.make_async_copy(block, slice_ref, sems.at[1])
    fetch.start()
    weight = mask_ref[place(COL) // 2, r].astype(jnp.float32).astype(jnp.bfloat16)
    load.wait()
    masked_ref[...] = masked_ref[...] * weight
    stores = [pltpu.make_async_copy(masked_ref.at[ring:], first_ref.at[batch_count:], sems.at[2])]
    for k in range(copies):
        stores.append(pltpu.make_async_copy(masked_ref.at[:ring], second_ref.at[k], sems.at[4 + k]))
    for store in stores:
        store.start()
    fetch.wait()
    rows = slice_ref[...].astype(jnp.float32)
    half = rows.shape[1] // 2
    for k in range(half // 4):
        for core in range(2):
            at = core * half + k * 4
            order_ref[:, at : at + 4, :] = rows[:, (2 * k + core) * 4 : (2 * k + core + 1) * 4, :]
    slice_ref[...] = order_ref[...].astype(jnp.bfloat16)
    stores.append(pltpu.make_async_copy(slice_ref, first_ref.at[:batch_count], sems.at[3]))
    stores[-1].start()
    for store in stores:
        store.wait()


def prepare_call(mask, amplitudes, factors, ring, copies):
    pair_count, rows, cols = amplitudes.shape
    flat = factors.shape[0] + pair_count - ring
    hbm = pl.BlockSpec(memory_space=pltpu.HBM)
    return pl.pallas_call(
        prepare_kernel,
        in_specs=[pl.BlockSpec(memory_space=pltpu.SMEM), hbm, hbm],
        out_specs=[hbm, hbm],
        out_shape=[
            jax.ShapeDtypeStruct((flat, rows, cols), jnp.bfloat16),
            jax.ShapeDtypeStruct((copies, ring, rows, cols), jnp.bfloat16),
        ],
        scratch_shapes=[
            pltpu.VMEM(amplitudes.shape, jnp.bfloat16),
            pltpu.VMEM((factors.shape[0], rows, cols), jnp.bfloat16),
            pltpu.VMEM((factors.shape[0], rows, cols), jnp.float32),
            pltpu.SemaphoreType.DMA((4 + copies,)),
        ],
        compiler_params=params(60),
    )(mask, amplitudes, factors)


def gate_kernel(held_ref, other_ref, out_ref):
    pass


def gate_call(held, other):
    anywhere = pl.BlockSpec(memory_space=pl.ANY)
    return pl.pallas_call(
        gate_kernel,
        in_specs=[anywhere, anywhere],
        out_specs=anywhere,
        out_shape=jax.ShapeDtypeStruct(held.shape, held.dtype),
        input_output_aliases={0: 0},
        compiler_params=params(),
    )(held, other)


def spread_product(product, out_ref, first, batch_count, block_rows):
    cols = out_ref.shape[0] // batch_count
    for pair in range(product.shape[1] // cols // 2):
        for q in range(batch_count):
            rows = product[q * block_rows : (q + 1) * block_rows, 2 * pair * cols : 2 * (pair + 1) * cols]
            block = jnp.concatenate([rows[:, :cols], rows[:, cols:]], axis=0)
            at = first + 2 * pair * block_rows
            out_ref[q * cols : (q + 1) * cols, at : at + 2 * block_rows] = block.T.astype(jnp.bfloat16)


def ring_term(own_ref, blocks, move):
    batch_count, block_rows, width = own_ref.shape
    group = width // 4
    at = pl.multiple_of(lax.rem(lax.axis_index("zh") + move, 4) * group, group)
    own = own_ref[:, :, pl.ds(at, group)].reshape(batch_count * block_rows, group)
    lanes = [
        jnp.concatenate([ref[k, p] for ref in blocks for k in range(ref.shape[0])], axis=0)
        for p in range(blocks[0].shape[1])
    ]
    return jnp.dot(own, jnp.concatenate(lanes, axis=1), preferred_element_type=jnp.float32)


def early_kernel(own_ref, near_ref, back_ref, ahead_ref, out_ref):
    step = 1 + 2 * lax.axis_index("zl")
    product = ring_term(own_ref, [near_ref], 0)
    product = product + ring_term(own_ref, [back_ref], 4 - step)
    out_ref[...] = product + ring_term(own_ref, [ahead_ref], step)


def early_call(own, parts):
    batch_count, block_rows, width = own.shape
    pair_count, rows, cols = parts[0].shape[1:]
    return pl.pallas_call(
        early_kernel,
        grid=(pair_count // 2,),
        in_specs=[pl.BlockSpec(memory_space=pltpu.VMEM)]
        + [pl.BlockSpec((part.shape[0], 2, rows, cols), lambda i: (0, i, 0, 0)) for part in parts],
        out_specs=pl.BlockSpec((batch_count * block_rows, 2 * cols), lambda i: (0, i)),
        out_shape=jax.ShapeDtypeStruct((batch_count * block_rows, pair_count * cols), jnp.float32),
        compiler_params=params(),
    )(own, *parts)


def late_kernel(own_ref, left_ref, right_ref, early_ref, out_ref):
    batch_count, block_rows, width = own_ref.shape
    product = early_ref[...] + ring_term(own_ref, [left_ref, right_ref], 2)
    spread_product(product, out_ref, 0, batch_count, block_rows)


def late_call(own, parts, early, total):
    batch_count, block_rows, width = own.shape
    pair_count, rows, cols = parts[0].shape[1:]
    vmem = pl.BlockSpec(memory_space=pltpu.VMEM)
    return pl.pallas_call(
        late_kernel,
        in_specs=[vmem] * 4,
        out_specs=vmem,
        out_shape=jax.ShapeDtypeStruct((batch_count * cols, total * block_rows), jnp.bfloat16),
        compiler_params=params(),
    )(own, *parts, early)


RING = ((0, 0, 4), (-1, 0, 4), (1, 0, 4), (-2, 0, 4), (2, 0, 4), (-3, 0, 4), (3, 0, 4), (4, 0, 2), (4, 2, 4))


def ring_place(move):
    return lax.rem(lax.axis_index("y") + 8 + move * (1 - 2 * lax.axis_index("core")), 8)


def flat_kernel(own_ref, held_ref, *refs):
    pieces, (out_ref, amps_ref, sems) = refs[: len(RING)], refs[len(RING) :]
    batch_count, block_rows, width = own_ref.shape
    y_count, z_count, pairs, rows, cols = amps_ref.shape
    loads = []
    for k, (move, first, last) in enumerate(RING):
        target = amps_ref.at[ring_place(move), pl.ds(first, last - first)]
        loads.append(pltpu.make_async_copy(pieces[k].at[:, pl.ds(batch_count, pairs)], target, sems.at[k]))
        loads[k].start()
    for load in loads:
        load.wait()
    lanes = [
        jnp.concatenate([amps_ref[y, z, p] for z in range(z_count) for y in range(y_count)], axis=0)
        for p in range(pairs)
    ]
    own = own_ref[...].reshape(batch_count * block_rows, width)
    product = jnp.dot(own, jnp.concatenate(lanes, axis=1), preferred_element_type=jnp.float32)
    spread_product(product, out_ref, out_ref.shape[1] - pairs * block_rows, batch_count, block_rows)


def flat_call(own, pieces, inner):
    batch_count, block_rows, width = own.shape
    z_count, unit_count, rows, cols = pieces[0].shape
    pairs = unit_count - batch_count
    vmem = pl.BlockSpec(memory_space=pltpu.VMEM)
    return pl.pallas_call(
        flat_kernel,
        in_specs=[vmem, vmem] + [pl.BlockSpec(memory_space=pl.ANY)] * len(pieces),
        out_specs=vmem,
        out_shape=jax.ShapeDtypeStruct(inner.shape, jnp.bfloat16),
        input_output_aliases={1: 0},
        scratch_shapes=[
            pltpu.VMEM((8, z_count, pairs, rows, cols), jnp.bfloat16),
            pltpu.SemaphoreType.DMA((len(pieces),)),
        ],
        compiler_params=params(),
    )(own, inner, *pieces)


def ladder_kernel(flip, inner_ref, *refs):
    pieces, (out_ref, block_ref, sems) = refs[: len(RING)], refs[len(RING) :]
    y_count, z_count, batch_count, rows, cols = block_ref.shape
    side = lax.rem(lax.axis_index("core") + flip, 2)
    step = z_count // 2
    here = pl.ds(pl.multiple_of(side * rows, rows), rows)
    loads = ([], [])
    for k in range(2):
        for m, (move, first, last) in enumerate(RING):
            if first <= k * step < last:
                source = pieces[m].at[pl.ds(k * step - first, step), pl.ds(0, batch_count), here]
                target = block_ref.at[ring_place(move), pl.ds(k * step, step)]
                loads[k].append(pltpu.make_async_copy(source, target, sems.at[k, m]))
                loads[k][-1].start()
    height = step * y_count * rows
    for k in range(2):
        for load in loads[k]:
            load.wait()
        places = [(z, y) for z in range(k * step, (k + 1) * step) for y in range(y_count)]
        lanes = [jnp.concatenate([block_ref[y, z, q] for z, y in places], axis=0) for q in range(batch_count)]
        factor = jnp.concatenate(lanes, axis=1)
        product = jnp.dot(factor, inner_ref[...], preferred_element_type=jnp.float32)
        out_ref[k * height : (k + 1) * height] = product.astype(out_ref.dtype)


def ladder_call(flip, inner, pieces, kind):
    depth, width = inner.shape
    z_count, unit_count, rows, cols = pieces[0].shape
    vmem = pl.BlockSpec(memory_space=pltpu.VMEM)
    return pl.pallas_call(
        functools.partial(ladder_kernel, flip),
        in_specs=[vmem] + [pl.BlockSpec(memory_space=pl.ANY)] * len(pieces),
        out_specs=vmem,
        out_shape=jax.ShapeDtypeStruct((8 * z_count * rows // 2, width), kind),
        scratch_shapes=[
            pltpu.VMEM((8, z_count, depth // cols, rows // 2, cols), jnp.bfloat16),
            pltpu.SemaphoreType.DMA((2, len(pieces))),
        ],
        compiler_params=params(),
    )(inner, *pieces)


def swing(block, axis):
    half = block.shape[axis] // 2
    first = lax.slice_in_dim(block, 0, half, axis=axis)
    return jnp.concatenate([lax.slice_in_dim(block, half, 2 * half, axis=axis), first], axis=axis)


def gather_kernel(keep_ref, other_ref, out_ref):
    groups, height, cols = out_ref.shape
    total = keep_ref[...] + other_ref[...].astype(jnp.float32)
    tiles = total.reshape(height // 8, 2, groups // 2, 8, cols)
    top = lax.broadcasted_iota(jnp.int32, (height // 8, 8, cols), 1) < 4
    for k in range(groups // 2):
        first, second = tiles[:, 0, k], tiles[:, 1, k]
        even = jnp.where(top, first, swing(second, 1))
        odd = jnp.where(top, swing(first, 1), second)
        out_ref[2 * k] = even.reshape(height, cols).astype(jnp.bfloat16)
        out_ref[2 * k + 1] = odd.reshape(height, cols).astype(jnp.bfloat16)


def gather_call(keep, other, groups):
    height, width = keep.shape
    cols = 128
    return pl.pallas_call(
        gather_kernel,
        grid=(width // cols,),
        in_specs=[pl.BlockSpec((height, cols), lambda i: (0, i))] * 2,
        out_specs=pl.BlockSpec((groups, height // groups, cols), lambda i: (0, 0, i)),
        out_shape=jax.ShapeDtypeStruct((groups, height // groups, width), jnp.bfloat16),
        compiler_params=params(),
    )(keep, other)


def reduce_kernel(mask_ref, part_ref, direct_ref, mirror_ref, stage_ref):
    sources, height, width = part_ref.shape
    cols = direct_ref.shape[3]
    half = cols // 2
    row = place(COL) // 2
    for k in range(width // cols):
        span = slice(k * cols, (k + 1) * cols)
        total = part_ref[0, :, span].astype(jnp.float32)
        for m in range(1, sources):
            total = total + part_ref[m, :, span].astype(jnp.float32)
        tiles = [total[t * 8 : (t + 1) * 8] * mask_ref[row, t].astype(jnp.float32) for t in range(height // 8)]
        total = jnp.concatenate(tiles, axis=0)
        tall = total.reshape(height // 8, 8, cols)
        stage_ref[:, 0, k * 4 : (k + 1) * 4, :] = tall[:, :4]
        stage_ref[:, 1, k * 4 : (k + 1) * 4, :] = tall[:, 4:]
        straight = total.T
        for m in range(2):
            p = 2 * k + m
            wide = straight[m * half : (m + 1) * half].reshape(half // 8, 8, height)
            direct_ref[:, 0, p * 4 : (p + 1) * 4, :] = wide[:, :4]
            direct_ref[:, 1, p * 4 : (p + 1) * 4, :] = wide[:, 4:]
    mirror_ref[...] = stage_ref[...].astype(jnp.bfloat16)


def reduce_call(mask, pieces):
    sources, height, width = pieces.shape
    cols = 128
    vmem = pl.BlockSpec(memory_space=pltpu.VMEM)
    groups = width // cols
    return pl.pallas_call(
        reduce_kernel,
        in_specs=[pl.BlockSpec(memory_space=pltpu.SMEM), vmem],
        out_specs=[vmem, vmem],
        out_shape=[
            jax.ShapeDtypeStruct((cols // 16, 2, groups * 8, height), jnp.float32),
            jax.ShapeDtypeStruct((height // 8, 2, groups * 4, cols), jnp.bfloat16),
        ],
        scratch_shapes=[pltpu.VMEM((height // 8, 2, groups * 4, cols), jnp.float32)],
        compiler_params=params(),
    )(mask, pieces)


def align_kernel(direct_ref, out_ref, rows_ref):
    height, width = out_ref.shape
    sources, _, cols = direct_ref.shape
    blocks, pack = width // cols, cols // height
    own_rows = cols // (2 * sources)
    for g in range(sources // pack):
        turned = direct_ref[g * pack : (g + 1) * pack].reshape(cols, cols).T
        for m in range(pack):
            at = (g * pack + m) * own_rows
            tall = turned[:, m * height : (m + 1) * height].reshape(blocks, 2 * own_rows, height)
            rows_ref[:, 0, at : at + own_rows, :] = tall[:, :own_rows]
            rows_ref[:, 1, at : at + own_rows, :] = tall[:, own_rows:]
    for k in range(blocks):
        out_ref[:, k * cols : (k + 1) * cols] = rows_ref[k].reshape(cols, height).T


def align_call(direct):
    sources, height, cols = direct.shape
    width = sources * cols
    vmem = pl.BlockSpec(memory_space=pltpu.VMEM)
    return pl.pallas_call(
        align_kernel,
        in_specs=[vmem],
        out_specs=vmem,
        out_shape=jax.ShapeDtypeStruct((height, width), jnp.float32),
        scratch_shapes=[pltpu.VMEM((width // cols, 2, cols // 2, height), jnp.float32)],
        compiler_params=params(),
    )(direct)


def combine_kernel(partner_ref, direct_ref, mirror_ref, out_ref):
    pair_count, own_rows, width = out_ref.shape
    cols = mirror_ref.shape[2]
    blocks = width // cols
    mirror = mirror_ref[...].astype(jnp.float32).reshape(blocks, 2, mirror_ref.shape[1], cols)
    early, late = mirror[:, 0], mirror[:, 1]
    front = lax.broadcasted_iota(jnp.int32, early.shape, 2) < cols // 2
    plain = jnp.where(front, early, swing(late, 2))
    moved = jnp.where(front, swing(early, 2), late)
    for p in range(pair_count):
        mate = partner_ref[p]
        chosen = jnp.where(lax.rem(mate, 2) == 1, moved, plain)
        picked = chosen[:, :own_rows]
        for k in range(1, pair_count // 2):
            picked = jnp.where(mate // 2 == k, chosen[:, k * own_rows : (k + 1) * own_rows], picked)
        for k in range(blocks):
            span = slice(k * cols, (k + 1) * cols)
            out_ref[p, :, span] = direct_ref[p * own_rows : (p + 1) * own_rows, span] + picked[k]


def combine_call(partner, direct, mirror, pair_count):
    height, width = direct.shape
    vmem = pl.BlockSpec(memory_space=pltpu.VMEM)
    return pl.pallas_call(
        combine_kernel,
        in_specs=[pl.BlockSpec(memory_space=pltpu.SMEM), vmem, vmem],
        out_specs=vmem,
        out_shape=jax.ShapeDtypeStruct((pair_count, height // pair_count, width), jnp.float32),
        compiler_params=params(),
    )(partner, direct, mirror)


def turn(count, step):
    return [(i, (i + step) % count) for i in range(count)]


def cross(count, step):
    return [(k, k // count * count + (k % count + (1 - k // count * 2) * step) % count) for k in range(2 * count)]


def on_device(amplitudes, factors, amp_mask, out_mask, partner):
    pair_count, amp_rows, amp_cols = amplitudes.shape
    batch_count, block_rows, full_width = factors.shape
    ring = 6
    first, second = prepare_call(amp_mask, amplitudes, factors, ring, 8)
    near = lax.all_to_all(second, "y", split_axis=0, concat_axis=0)
    held = gate_call(lax.all_gather(first, "zh", axis=0), near)

    back = lax.ppermute(near, ("zl", "zh"), cross(4, 1))
    ahead = lax.ppermute(near, ("zl", "zh"), cross(4, -1))
    left = lax.ppermute(back[:4], ("zl", "zh"), cross(4, 1))
    right = lax.ppermute(ahead[4:], ("zl", "zh"), cross(4, -1))

    up, down = held, held
    units = [held]
    for k in range(3):
        up = lax.ppermute(up, ("core", "y"), cross(8, 1))
        down = lax.ppermute(down, ("core", "y"), cross(8, -1))
        if k == 1:
            up = gate_call(up, ahead)
        if k == 2:
            up = gate_call(up, back)
        units += [up, down]
    units.append(lax.ppermute(up[:2], ("core", "y"), cross(8, 1)))
    units.append(lax.ppermute(down[2:], ("core", "y"), cross(8, -1)))

    early = early_call(factors, (near, back, ahead))
    late = late_call(factors, (left, right), early, pair_count)
    inner = flat_call(factors, units, late)
    swapped = lax.ppermute(ladder_call(1, inner, units, jnp.bfloat16), "core", turn(2, 1))
    keep = ladder_call(0, inner, units, jnp.float32)
    partial = gather_call(keep, swapped, 8)
    pieces = lax.all_to_all(partial, ("zl", "x"), split_axis=0, concat_axis=0)
    direct, mirror = reduce_call(out_mask, pieces)
    mirror = lax.all_to_all(mirror.reshape(32, 16, 128), COL, split_axis=0, concat_axis=0)
    direct = lax.all_to_all(direct.reshape(16, 32, 128), ROW, split_axis=0, concat_axis=0)
    return combine_call(partner, align_call(direct), mirror, pair_count)


def solution(mesh):
    fine = Mesh(mesh.devices.reshape(2, 4, 2, 4, 8), ALL)
    return jax.shard_map(
        on_device,
        mesh=fine,
        in_specs=(P(None, COL, ROW), P(None, COL, None), P(), P(), P()),
        out_specs=P(None, COL + ROW, None),
        check_vma=False,
    )
```

```python
import functools

import jax
import jax.numpy as jnp
from jax import lax
from jax.experimental import pallas as pl
from jax.experimental.pallas import tpu as pltpu
from jax.sharding import Mesh, PartitionSpec as P

ROW = ("zl", "x", "core")
COL = ("zh", "y")
ALL = ROW + COL
MIB = 1024 * 1024


def params(mib=16):
    return pltpu.CompilerParams(vmem_limit_bytes=mib * MIB)


def place(names):
    at = lax.axis_index(names[0])
    for name in names[1:]:
        at = at * lax.axis_size(name) + lax.axis_index(name)
    return at


def prepare_kernel(mask_ref, amps_ref, factor_ref, first_ref, second_ref, masked_ref, slice_ref, order_ref, sems):
    batch_count, (copies, ring) = factor_ref.shape[0], second_ref.shape[:2]
    r = place(ROW)
    cols = amps_ref.shape[2]
    load = pltpu.make_async_copy(amps_ref, masked_ref, sems.at[0])
    load.start()
    block = factor_ref.at[:, :, pl.ds(pl.multiple_of(r * cols, cols), cols)]
    fetch = pltpu.make_async_copy(block, slice_ref, sems.at[1])
    fetch.start()
    weight = mask_ref[place(COL) // 2, r].astype(jnp.float32).astype(jnp.bfloat16)
    load.wait()
    masked_ref[...] = masked_ref[...] * weight
    stores = [pltpu.make_async_copy(masked_ref.at[ring:], first_ref.at[batch_count:], sems.at[2])]
    for k in range(copies):
        stores.append(pltpu.make_async_copy(masked_ref.at[:ring], second_ref.at[k], sems.at[4 + k]))
    for store in stores:
        store.start()
    fetch.wait()
    rows = slice_ref[...].astype(jnp.float32)
    half = rows.shape[1] // 2
    for k in range(half // 4):
        for core in range(2):
            at = core * half + k * 4
            order_ref[:, at : at + 4, :] = rows[:, (2 * k + core) * 4 : (2 * k + core + 1) * 4, :]
    slice_ref[...] = order_ref[...].astype(jnp.bfloat16)
    stores.append(pltpu.make_async_copy(slice_ref, first_ref.at[:batch_count], sems.at[3]))
    stores[-1].start()
    for store in stores:
        store.wait()


def prepare_call(mask, amplitudes, factors, ring, copies):
    pair_count, rows, cols = amplitudes.shape
    flat = factors.shape[0] + pair_count - ring
    hbm = pl.BlockSpec(memory_space=pltpu.HBM)
    return pl.pallas_call(
        prepare_kernel,
        in_specs=[pl.BlockSpec(memory_space=pltpu.SMEM), hbm, hbm],
        out_specs=[hbm, hbm],
        out_shape=[
            jax.ShapeDtypeStruct((flat, rows, cols), jnp.bfloat16),
            jax.ShapeDtypeStruct((copies, ring, rows, cols), jnp.bfloat16),
        ],
        scratch_shapes=[
            pltpu.VMEM(amplitudes.shape, jnp.bfloat16),
            pltpu.VMEM((factors.shape[0], rows, cols), jnp.bfloat16),
            pltpu.VMEM((factors.shape[0], rows, cols), jnp.float32),
            pltpu.SemaphoreType.DMA((4 + copies,)),
        ],
        compiler_params=params(60),
    )(mask, amplitudes, factors)


def gate_kernel(held_ref, other_ref, out_ref):
    pass


def gate_call(held, other):
    anywhere = pl.BlockSpec(memory_space=pl.ANY)
    return pl.pallas_call(
        gate_kernel,
        in_specs=[anywhere, anywhere],
        out_specs=anywhere,
        out_shape=jax.ShapeDtypeStruct(held.shape, held.dtype),
        input_output_aliases={0: 0},
        compiler_params=params(),
    )(held, other)


def spread_product(product, out_ref, first, batch_count, block_rows):
    cols = out_ref.shape[0] // batch_count
    for pair in range(product.shape[1] // cols // 2):
        for q in range(batch_count):
            rows = product[q * block_rows : (q + 1) * block_rows, 2 * pair * cols : 2 * (pair + 1) * cols]
            block = jnp.concatenate([rows[:, :cols], rows[:, cols:]], axis=0)
            at = first + 2 * pair * block_rows
            out_ref[q * cols : (q + 1) * cols, at : at + 2 * block_rows] = block.T.astype(jnp.bfloat16)


def ring_term(own_ref, blocks, move):
    batch_count, block_rows, width = own_ref.shape
    group = width // 4
    at = pl.multiple_of(lax.rem(lax.axis_index("zh") + move, 4) * group, group)
    own = own_ref[:, :, pl.ds(at, group)].reshape(batch_count * block_rows, group)
    lanes = [
        jnp.concatenate([ref[k, p] for ref in blocks for k in range(ref.shape[0])], axis=0)
        for p in range(blocks[0].shape[1])
    ]
    return jnp.dot(own, jnp.concatenate(lanes, axis=1), preferred_element_type=jnp.float32)


def early_kernel(own_ref, near_ref, back_ref, ahead_ref, out_ref):
    step = 1 + 2 * lax.axis_index("core")
    product = ring_term(own_ref, [near_ref], 0)
    product = product + ring_term(own_ref, [back_ref], 4 - step)
    out_ref[...] = product + ring_term(own_ref, [ahead_ref], step)


def early_call(own, parts):
    batch_count, block_rows, width = own.shape
    pair_count, rows, cols = parts[0].shape[1:]
    return pl.pallas_call(
        early_kernel,
        grid=(pair_count // 2,),
        in_specs=[pl.BlockSpec(memory_space=pltpu.VMEM)]
        + [pl.BlockSpec((part.shape[0], 2, rows, cols), lambda i: (0, i, 0, 0)) for part in parts],
        out_specs=pl.BlockSpec((batch_count * block_rows, 2 * cols), lambda i: (0, i)),
        out_shape=jax.ShapeDtypeStruct((batch_count * block_rows, pair_count * cols), jnp.float32),
        compiler_params=params(),
    )(own, *parts)


def late_kernel(own_ref, left_ref, right_ref, early_ref, out_ref):
    batch_count, block_rows, width = own_ref.shape
    product = early_ref[...] + ring_term(own_ref, [left_ref, right_ref], 2)
    spread_product(product, out_ref, 0, batch_count, block_rows)


def late_call(own, parts, early, total):
    batch_count, block_rows, width = own.shape
    pair_count, rows, cols = parts[0].shape[1:]
    vmem = pl.BlockSpec(memory_space=pltpu.VMEM)
    return pl.pallas_call(
        late_kernel,
        in_specs=[vmem] * 4,
        out_specs=vmem,
        out_shape=jax.ShapeDtypeStruct((batch_count * cols, total * block_rows), jnp.bfloat16),
        compiler_params=params(),
    )(own, *parts, early)


RING = ((0, 0, 4), (-1, 0, 4), (1, 0, 4), (-2, 0, 4), (2, 0, 4), (-3, 0, 4), (3, 0, 4), (4, 0, 2), (4, 2, 4))


def ring_place(move):
    return lax.rem(lax.axis_index("y") + 8 + move * (1 - 2 * lax.axis_index("core")), 8)


def flat_kernel(own_ref, held_ref, *refs):
    pieces, (out_ref, amps_ref, sems) = refs[: len(RING)], refs[len(RING) :]
    batch_count, block_rows, width = own_ref.shape
    y_count, z_count, pairs, rows, cols = amps_ref.shape
    loads = []
    for k, (move, first, last) in enumerate(RING):
        target = amps_ref.at[ring_place(move), pl.ds(first, last - first)]
        loads.append(pltpu.make_async_copy(pieces[k].at[:, pl.ds(batch_count, pairs)], target, sems.at[k]))
        loads[k].start()
    for load in loads:
        load.wait()
    lanes = [
        jnp.concatenate([amps_ref[y, z, p] for z in range(z_count) for y in range(y_count)], axis=0)
        for p in range(pairs)
    ]
    own = own_ref[...].reshape(batch_count * block_rows, width)
    product = jnp.dot(own, jnp.concatenate(lanes, axis=1), preferred_element_type=jnp.float32)
    spread_product(product, out_ref, out_ref.shape[1] - pairs * block_rows, batch_count, block_rows)


def flat_call(own, pieces, inner):
    batch_count, block_rows, width = own.shape
    z_count, unit_count, rows, cols = pieces[0].shape
    pairs = unit_count - batch_count
    vmem = pl.BlockSpec(memory_space=pltpu.VMEM)
    return pl.pallas_call(
        flat_kernel,
        in_specs=[vmem, vmem] + [pl.BlockSpec(memory_space=pl.ANY)] * len(pieces),
        out_specs=vmem,
        out_shape=jax.ShapeDtypeStruct(inner.shape, jnp.bfloat16),
        input_output_aliases={1: 0},
        scratch_shapes=[
            pltpu.VMEM((8, z_count, pairs, rows, cols), jnp.bfloat16),
            pltpu.SemaphoreType.DMA((len(pieces),)),
        ],
        compiler_params=params(),
    )(own, inner, *pieces)


def ladder_kernel(flip, inner_ref, *refs):
    pieces, (out_ref, block_ref, sems) = refs[: len(RING)], refs[len(RING) :]
    y_count, z_count, batch_count, rows, cols = block_ref.shape
    side = lax.rem(lax.axis_index("core") + flip, 2)
    step = z_count // 2
    here = pl.ds(pl.multiple_of(side * rows, rows), rows)
    loads = ([], [])
    for k in range(2):
        for m, (move, first, last) in enumerate(RING):
            if first <= k * step < last:
                source = pieces[m].at[pl.ds(k * step - first, step), pl.ds(0, batch_count), here]
                target = block_ref.at[ring_place(move), pl.ds(k * step, step)]
                loads[k].append(pltpu.make_async_copy(source, target, sems.at[k, m]))
                loads[k][-1].start()
    height = step * y_count * rows
    for k in range(2):
        for load in loads[k]:
            load.wait()
        places = [(z, y) for z in range(k * step, (k + 1) * step) for y in range(y_count)]
        lanes = [jnp.concatenate([block_ref[y, z, q] for z, y in places], axis=0) for q in range(batch_count)]
        factor = jnp.concatenate(lanes, axis=1)
        product = jnp.dot(factor, inner_ref[...], preferred_element_type=jnp.float32)
        out_ref[k * height : (k + 1) * height] = product.astype(out_ref.dtype)


def ladder_call(flip, inner, pieces, kind):
    depth, width = inner.shape
    z_count, unit_count, rows, cols = pieces[0].shape
    vmem = pl.BlockSpec(memory_space=pltpu.VMEM)
    return pl.pallas_call(
        functools.partial(ladder_kernel, flip),
        in_specs=[vmem] + [pl.BlockSpec(memory_space=pl.ANY)] * len(pieces),
        out_specs=vmem,
        out_shape=jax.ShapeDtypeStruct((8 * z_count * rows // 2, width), kind),
        scratch_shapes=[
            pltpu.VMEM((8, z_count, depth // cols, rows // 2, cols), jnp.bfloat16),
            pltpu.SemaphoreType.DMA((2, len(pieces))),
        ],
        compiler_params=params(),
    )(inner, *pieces)


def swing(block, axis):
    half = block.shape[axis] // 2
    first = lax.slice_in_dim(block, 0, half, axis=axis)
    return jnp.concatenate([lax.slice_in_dim(block, half, 2 * half, axis=axis), first], axis=axis)


def gather_kernel(keep_ref, other_ref, out_ref):
    groups, height, cols = out_ref.shape
    total = keep_ref[...] + other_ref[...].astype(jnp.float32)
    tiles = total.reshape(height // 8, 2, groups // 2, 8, cols)
    top = lax.broadcasted_iota(jnp.int32, (height // 8, 8, cols), 1) < 4
    for k in range(groups // 2):
        first, second = tiles[:, 0, k], tiles[:, 1, k]
        even = jnp.where(top, first, swing(second, 1))
        odd = jnp.where(top, swing(first, 1), second)
        out_ref[2 * k] = even.reshape(height, cols).astype(jnp.bfloat16)
        out_ref[2 * k + 1] = odd.reshape(height, cols).astype(jnp.bfloat16)


def gather_call(keep, other, groups):
    height, width = keep.shape
    cols = 128
    return pl.pallas_call(
        gather_kernel,
        grid=(width // cols,),
        in_specs=[pl.BlockSpec((height, cols), lambda i: (0, i))] * 2,
        out_specs=pl.BlockSpec((groups, height // groups, cols), lambda i: (0, 0, i)),
        out_shape=jax.ShapeDtypeStruct((groups, height // groups, width), jnp.bfloat16),
        compiler_params=params(),
    )(keep, other)


def reduce_kernel(mask_ref, part_ref, direct_ref, mirror_ref, stage_ref):
    sources, height, width = part_ref.shape
    cols = direct_ref.shape[3]
    half = cols // 2
    row = place(COL) // 2
    for k in range(width // cols):
        span = slice(k * cols, (k + 1) * cols)
        total = part_ref[0, :, span].astype(jnp.float32)
        for m in range(1, sources):
            total = total + part_ref[m, :, span].astype(jnp.float32)
        tiles = [total[t * 8 : (t + 1) * 8] * mask_ref[row, t].astype(jnp.float32) for t in range(height // 8)]
        total = jnp.concatenate(tiles, axis=0)
        tall = total.reshape(height // 8, 8, cols)
        stage_ref[:, 0, k * 4 : (k + 1) * 4, :] = tall[:, :4]
        stage_ref[:, 1, k * 4 : (k + 1) * 4, :] = tall[:, 4:]
        straight = total.T
        for m in range(2):
            p = 2 * k + m
            wide = straight[m * half : (m + 1) * half].reshape(half // 8, 8, height)
            direct_ref[:, 0, p * 4 : (p + 1) * 4, :] = wide[:, :4]
            direct_ref[:, 1, p * 4 : (p + 1) * 4, :] = wide[:, 4:]
    mirror_ref[...] = stage_ref[...].astype(jnp.bfloat16)


def reduce_call(mask, pieces):
    sources, height, width = pieces.shape
    cols = 128
    vmem = pl.BlockSpec(memory_space=pltpu.VMEM)
    groups = width // cols
    return pl.pallas_call(
        reduce_kernel,
        in_specs=[pl.BlockSpec(memory_space=pltpu.SMEM), vmem],
        out_specs=[vmem, vmem],
        out_shape=[
            jax.ShapeDtypeStruct((cols // 16, 2, groups * 8, height), jnp.float32),
            jax.ShapeDtypeStruct((height // 8, 2, groups * 4, cols), jnp.bfloat16),
        ],
        scratch_shapes=[pltpu.VMEM((height // 8, 2, groups * 4, cols), jnp.float32)],
        compiler_params=params(),
    )(mask, pieces)


def align_kernel(direct_ref, out_ref, rows_ref):
    height, width = out_ref.shape
    sources, _, cols = direct_ref.shape
    blocks, pack = width // cols, cols // height
    own_rows = cols // (2 * sources)
    for g in range(sources // pack):
        turned = direct_ref[g * pack : (g + 1) * pack].reshape(cols, cols).T
        for m in range(pack):
            at = (g * pack + m) * own_rows
            tall = turned[:, m * height : (m + 1) * height].reshape(blocks, 2 * own_rows, height)
            rows_ref[:, 0, at : at + own_rows, :] = tall[:, :own_rows]
            rows_ref[:, 1, at : at + own_rows, :] = tall[:, own_rows:]
    for k in range(blocks):
        out_ref[:, k * cols : (k + 1) * cols] = rows_ref[k].reshape(cols, height).T


def align_call(direct):
    sources, height, cols = direct.shape
    width = sources * cols
    vmem = pl.BlockSpec(memory_space=pltpu.VMEM)
    return pl.pallas_call(
        align_kernel,
        in_specs=[vmem],
        out_specs=vmem,
        out_shape=jax.ShapeDtypeStruct((height, width), jnp.float32),
        scratch_shapes=[pltpu.VMEM((width // cols, 2, cols // 2, height), jnp.float32)],
        compiler_params=params(),
    )(direct)


def combine_kernel(partner_ref, direct_ref, mirror_ref, out_ref):
    pair_count, own_rows, width = out_ref.shape
    cols = mirror_ref.shape[2]
    blocks = width // cols
    mirror = mirror_ref[...].astype(jnp.float32).reshape(blocks, 2, mirror_ref.shape[1], cols)
    early, late = mirror[:, 0], mirror[:, 1]
    front = lax.broadcasted_iota(jnp.int32, early.shape, 2) < cols // 2
    plain = jnp.where(front, early, swing(late, 2))
    moved = jnp.where(front, swing(early, 2), late)
    for p in range(pair_count):
        mate = partner_ref[p]
        chosen = jnp.where(lax.rem(mate, 2) == 1, moved, plain)
        picked = chosen[:, :own_rows]
        for k in range(1, pair_count // 2):
            picked = jnp.where(mate // 2 == k, chosen[:, k * own_rows : (k + 1) * own_rows], picked)
        for k in range(blocks):
            span = slice(k * cols, (k + 1) * cols)
            out_ref[p, :, span] = direct_ref[p * own_rows : (p + 1) * own_rows, span] + picked[k]


def combine_call(partner, direct, mirror, pair_count):
    height, width = direct.shape
    vmem = pl.BlockSpec(memory_space=pltpu.VMEM)
    return pl.pallas_call(
        combine_kernel,
        in_specs=[pl.BlockSpec(memory_space=pltpu.SMEM), vmem, vmem],
        out_specs=vmem,
        out_shape=jax.ShapeDtypeStruct((pair_count, height // pair_count, width), jnp.float32),
        compiler_params=params(),
    )(partner, direct, mirror)


def turn(count, step):
    return [(i, (i + step) % count) for i in range(count)]


def cross(count, step):
    return [(k, k // count * count + (k % count + (1 - k // count * 2) * step) % count) for k in range(2 * count)]


def on_device(amplitudes, factors, amp_mask, out_mask, partner):
    pair_count, amp_rows, amp_cols = amplitudes.shape
    batch_count, block_rows, full_width = factors.shape
    ring = 6
    first, second = prepare_call(amp_mask, amplitudes, factors, ring, 8)
    near = lax.all_to_all(second, "y", split_axis=0, concat_axis=0)
    held = gate_call(lax.all_gather(first, "zh", axis=0), near)

    back = lax.ppermute(near, ("core", "zh"), cross(4, 1))
    ahead = lax.ppermute(near, ("core", "zh"), cross(4, -1))
    left = lax.ppermute(back[:4], ("core", "zh"), cross(4, 1))
    right = lax.ppermute(ahead[4:], ("core", "zh"), cross(4, -1))

    up, down = held, held
    units = [held]
    for k in range(3):
        up = lax.ppermute(up, ("core", "y"), cross(8, 1))
        down = lax.ppermute(down, ("core", "y"), cross(8, -1))
        if k == 1:
            up = gate_call(up, ahead)
        if k == 2:
            up = gate_call(up, back)
        units += [up, down]
    units.append(lax.ppermute(up[:2], ("core", "y"), cross(8, 1)))
    units.append(lax.ppermute(down[2:], ("core", "y"), cross(8, -1)))

    early = early_call(factors, (near, back, ahead))
    late = late_call(factors, (left, right), early, pair_count)
    inner = flat_call(factors, units, late)
    swapped = lax.ppermute(ladder_call(1, inner, units, jnp.bfloat16), "core", turn(2, 1))
    keep = ladder_call(0, inner, units, jnp.float32)
    partial = gather_call(keep, swapped, 8)
    pieces = lax.all_to_all(partial, ("zl", "x"), split_axis=0, concat_axis=0)
    direct, mirror = reduce_call(out_mask, pieces)
    mirror = lax.all_to_all(mirror.reshape(32, 16, 128), COL, split_axis=0, concat_axis=0)
    direct = lax.all_to_all(direct.reshape(16, 32, 128), ROW, split_axis=0, concat_axis=0)
    return combine_call(partner, align_call(direct), mirror, pair_count)


def solution(mesh):
    fine = Mesh(mesh.devices.reshape(2, 4, 2, 4, 8), ALL)
    return jax.shard_map(
        on_device,
        mesh=fine,
        in_specs=(P(None, COL, ROW), P(None, COL, None), P(), P(), P()),
        out_specs=P(None, COL + ROW, None),
        check_vma=False,
    )
```
